256 devices in a mesh: seq: 64 (over y, z, core), head: 4 (over x).
Axes of the slice: x: 4, y: 4, z: 8, core: 2. Of those that a mesh axis runs over, the one named last changes fastest.
Arguments:
- queries: bfloat16 [12288, 4096], P('seq', 'head'), may hold values from -10 to 10
- key_states: bfloat16 [12288, 1024], P('seq', 'head'), may hold values from -6 to 6
- value_states: bfloat16 [12288, 1024], P('seq', 'head'), may hold values from -6 to 6
- out_weight: bfloat16 [4096, 4096], P('head'), may hold values from -0.09375 to 0.09375
Outputs:
- mixed: bfloat16 [12288, 4096], P('seq', 'head')
The draws below stay inside these ranges and needn't reach their ends.
All inputs are finite; a program needn't handle non-finite values.
Results may differ from the reference program's by a relative error of at most 0.02.
Values may be sent and summed in bfloat16 or wider, within the bound.
A program may use at most 128 MiB of HBM per device.

```python
import jax
import jax.numpy as jnp
from jax import lax

D = 4096
HEADS = 32
KV_HEADS = 8
HEAD_DIM = 128
T_DEV = 192
SEQ = 12288


def draw_queries(key, part):
    key = jax.random.fold_in(key, 1)
    grouping = HEADS // KV_HEADS
    base = jnp.clip(2.5 * jax.random.normal(key, (SEQ, KV_HEADS, grouping, HEAD_DIM), jnp.float32), -10.0, 10.0)
    return base.reshape(SEQ, HEADS * HEAD_DIM).astype(jnp.bfloat16)


def draw_key_states(key, part):
    key = jax.random.fold_in(key, 2)
    base = jnp.clip(jax.random.normal(key, (SEQ, KV_HEADS, HEAD_DIM), jnp.float32), -6.0, 6.0)
    return base.reshape(SEQ, KV_HEADS * HEAD_DIM).astype(jnp.bfloat16)


def block_levels(key, dims, split, least, top_value):
    loudness = 1.0
    for position, blocks in split:
        steps = jax.random.uniform(jax.random.fold_in(jax.random.fold_in(key, 6), position), (blocks,), jnp.float32, least / len(split), top_value / len(split))
        loudness = loudness * jnp.repeat(jnp.exp(steps), dims[position] // blocks).reshape((-1,) + (1,) * (len(dims) - 1 - position))
    return loudness


def bell_draw(rng, shape, scale, most, pieces=(), held_as=jnp.bfloat16):
    array = jax.random.normal(rng, shape, jnp.float32) * scale
    if len(pieces) > 0:
        array = block_levels(rng, shape, pieces, -0.22, 0.18) * array
    return jnp.clip(array, min=-most, max=most).astype(held_as)


def setup_inputs(seed: int = 0) -> dict:
    seeds = jax.random.split(jax.random.key(seed), 5)
    return {
        "queries": draw_queries(jax.random.fold_in(seeds[4], 71), 0),
        "key_states": draw_key_states(jax.random.fold_in(seeds[4], 71), 0),
        "value_states": bell_draw(seeds[2], (SEQ, KV_HEADS * HEAD_DIM), 1.0, 6.0, ((0, 64), (1, 4))),
        "out_weight": bell_draw(seeds[3], (HEADS * HEAD_DIM, D), (HEADS * HEAD_DIM) ** -0.5, 0.09375, ((0, 4),)),
    }


def reference(queries, key_states, value_states, out_weight):
    length = queries.shape[0]
    grouping = HEADS // KV_HEADS
    scale = HEAD_DIM ** -0.5
    query_heads = queries.reshape(length, KV_HEADS, grouping, HEAD_DIM)
    key_heads = key_states.reshape(length, KV_HEADS, HEAD_DIM)
    value_heads = value_states.reshape(length, KV_HEADS, HEAD_DIM)
    blocks = length // T_DEV
    positions = jnp.arange(length, dtype=jnp.int32)
    block_list = jnp.repeat(jnp.arange(blocks, dtype=jnp.int32), KV_HEADS)
    head_list = jnp.tile(jnp.arange(KV_HEADS, dtype=jnp.int32), blocks)

    def one_task(task):
        block_num, head_num = task
        start = (block_num * T_DEV).astype(jnp.int32)
        query_block = lax.dynamic_slice_in_dim(query_heads, start, T_DEV, 0)
        query_block = lax.dynamic_index_in_dim(query_block, head_num, 1, keepdims=False)
        key_head = lax.dynamic_index_in_dim(key_heads, head_num, 1, keepdims=False)
        value_head = lax.dynamic_index_in_dim(value_heads, head_num, 1, keepdims=False)
        scores = jnp.einsum("tgd,sd->tgs", query_block.astype(jnp.float32), key_head.astype(jnp.float32)) * scale
        query_pos = start + jnp.arange(T_DEV, dtype=jnp.int32)
        allowed = (positions[None, :] <= query_pos[:, None])[:, None, :]
        scores = jnp.where(allowed, scores, -jnp.inf)
        highest = jnp.max(scores, axis=2, keepdims=True)
        weights = jnp.where(allowed, jnp.exp(scores - highest), 0.0)
        total = jnp.sum(weights, axis=2)
        rounded = lax.optimization_barrier(weights.astype(jnp.bfloat16)).astype(jnp.float32)
        numerator = jnp.einsum("tgs,sd->tgd", rounded, value_head.astype(jnp.float32))
        return numerator / total[:, :, None]

    results = lax.map(one_task, (block_list, head_list))
    results = results.reshape(blocks, KV_HEADS, T_DEV, grouping, HEAD_DIM).transpose(0, 2, 1, 3, 4)
    attended = results.reshape(length, HEADS * HEAD_DIM).astype(jnp.bfloat16)
    return jnp.dot(attended, out_weight, preferred_element_type=jnp.float32).astype(jnp.bfloat16)
```

```python
import jax
import jax.numpy as jnp
from jax import lax
from jax.experimental import pallas as pl
from jax.experimental.pallas import tpu as pltpu
from jax.sharding import PartitionSpec as P

MESH = pl.DeviceIdType.MESH
HEAD_DIM = 128
SCALE = HEAD_DIM ** -0.5 * 1.4426950408889634
NEG = -1e30
T = 192
U = 2 * T
Z = 8
ROWS = 2 * U
TILE = 256


def kernel(
    q_ref, k_ref, v_ref, w_ref, out_ref,
    kv, qraw, qs, acc, top, att, attin, wv, po, pp, pm, ro, fp, fm,
    r_sem, s_sem, sr_sem, ss_sem, ys_sem, own_sem, part_r, part_s,
    q_own, q_r, q_s, w_sem, att_r, att_s, att_own, x_r, x_s,
):
    seq, x = lax.axis_index("seq"), lax.axis_index("head")
    y, z, c = seq // 16, (seq // 2) % Z, seq % 2
    late_home = y // 2
    h = late_home
    outer = jnp.where((y == 0) | (y == 3), 1, 0)
    inner = 1 - outer
    z_up, z_down = (z + 1) % Z, (z + Z - 1) % Z
    y_near = y + 1 - 2 * (y % 2)
    y_pair = 3 - y
    xp, xm, xo = (x + 1) % 4, (x + 3) % 4, (x + 2) % 4

    def dev(yy, zz, cc, xx=None):
        return ((yy * Z + zz) * 2 + cc, x if xx is None else xx)

    up, down = dev(y, z_up, c), dev(y, z_down, c)
    near, sibling = dev(y_near, z, c), dev(y, z, 1 - c)
    pair, pair_cross = dev(y_pair, z, c), dev(y_pair, z, 1 - c)
    x_up, x_down = dev(y, z, c, xp), dev(y, z, c, xm)

    barrier = pltpu.get_barrier_semaphore()
    for other in (up, down, near, sibling, pair, pair_cross, x_up, x_down):
        pl.semaphore_signal(barrier, inc=1, device_id=other, device_id_type=MESH)

    mine = pl.ds(pl.multiple_of(c * T, T), T)

    def block(slot, zz):
        return kv.at[slot, zz, :, mine, :]

    def half(slot, zz, which):
        return kv.at[slot, zz, which, mine, :]

    def remote(src, dst, s, r, to):
        return pltpu.make_async_remote_copy(
            src_ref=src, dst_ref=dst, send_sem=s, recv_sem=r, device_id=to, device_id_type=MESH
        )

    own_slot = 2 * late_home
    other_slot = 2 - own_slot
    own_copies = [
        pltpu.make_async_copy(
            ref.at[:, pl.ds(pl.multiple_of(h * HEAD_DIM, HEAD_DIM), HEAD_DIM)],
            half(own_slot, z, i),
            own_sem.at[i],
        )
        for i, ref in enumerate((k_ref, v_ref))
    ]
    for copy in own_copies:
        copy.start()

    def q_cols(hh, cc):
        return q_ref.at[:, pl.ds(pl.multiple_of(hh * 512 + cc * 256, 256), 256)]

    my_q = pltpu.make_async_copy(q_cols(h, c), qraw.at[late_home, mine, :], q_own)
    my_q.start()
    pl.semaphore_wait(barrier, 8)

    pair_copies = [
        remote(
            ref.at[:, pl.ds(pl.multiple_of((1 - h) * HEAD_DIM, HEAD_DIM), HEAD_DIM)],
            half(own_slot, z, i),
            part_s.at[i],
            part_r.at[i],
            pair,
        )
        for i, ref in enumerate((k_ref, v_ref))
    ]
    for copy in pair_copies:
        copy.start()
    q_copies = [
        remote(q_cols(h, 1 - c), qraw.at[late_home, mine, :], q_s.at[0], q_r.at[0], sibling),
        remote(q_cols(1 - h, c), qraw.at[late_home, mine, :], q_s.at[1], q_r.at[1], pair),
        remote(q_cols(1 - h, 1 - c), qraw.at[late_home, mine, :], q_s.at[2], q_r.at[2], pair_cross),
    ]
    for copy in q_copies:
        copy.start()
    w_copies = [
        pltpu.make_async_copy(
            w_ref.at[:, pl.ds(pl.multiple_of(col * 1024, 1024), 1024)], wv.at[j], w_sem.at[j]
        )
        for j, col in enumerate((xo, xp, xm, x))
    ]
    for copy in w_copies:
        copy.start()

    def hop(slot, zz, msg, to):
        return remote(block(slot, zz), block(slot, zz), s_sem.at[slot, msg], r_sem.at[slot, msg], to)

    def hop_half(slot, zz, which, msg, to):
        return remote(
            half(slot, zz, which), half(slot, zz, which), s_sem.at[slot, msg], r_sem.at[slot, msg], to
        )

    def to_sibling(slot, zz, msg):
        return remote(block(slot, zz), block(slot, zz), ss_sem.at[slot, msg], sr_sem.at[slot, msg], sibling)

    def to_sibling_half(slot, zz, which, msg):
        return remote(
            half(slot, zz, which), half(slot, zz, which), ss_sem.at[slot, msg], sr_sem.at[slot, msg], sibling
        )

    def to_near(zz, msg):
        return remote(block(0, zz), block(1, zz), ys_sem.at[msg], r_sem.at[1, msg], near)

    def to_near_half(zz, which, msg):
        return remote(half(0, zz, which), half(1, zz, which), ys_sem.at[msg], r_sem.at[1, msg], near)

    def late_to_near():
        return remote(block(2, z), block(3, z), ys_sem.at[9], r_sem.at[3, 0], near)

    def from_sibling(slot, zz, msg):
        theirs = pl.ds(pl.multiple_of((1 - c) * T, T), T)
        ref = kv.at[slot, zz, :, theirs, :]
        return remote(ref, ref, ss_sem.at[slot, msg], sr_sem.at[slot, msg], sibling)

    def from_sibling_half(slot, zz, which, msg):
        theirs = pl.ds(pl.multiple_of((1 - c) * T, T), T)
        ref = kv.at[slot, zz, which, theirs, :]
        return remote(ref, ref, ss_sem.at[slot, msg], sr_sem.at[slot, msg], sibling)

    def below(k):
        return (z + Z - k) % Z

    def above(k):
        return (z + k) % Z

    def start_own(slot):
        hop(slot, z, 1, up).start()
        hop(slot, z, 5, down).start()
        to_sibling(slot, z, 0).start()

    for copy in own_copies:
        copy.wait()
    start_own(own_slot)

    @pl.when(late_home == 0)
    def _():
        to_near(z, 0).start()

    @pl.when((late_home == 1) & (inner == 1))
    def _():
        late_to_near().start()

    for i in range(2):
        remote(half(other_slot, z, i), half(other_slot, z, i), part_s.at[i], part_r.at[i], pair).wait_recv()
    start_own(other_slot)

    @pl.when(late_home == 1)
    def _():
        to_near(z, 0).start()

    @pl.when((late_home == 0) & (inner == 1))
    def _():
        late_to_near().start()

    acc[...] = jnp.zeros_like(acc)
    top[...] = jnp.full_like(top, NEG)

    def prepare(group):
        for head in range(2):
            value = qraw[group, :, head * 128 : (head + 1) * 128].astype(jnp.float32) * SCALE
            high = value.astype(jnp.bfloat16)
            low = (value - high.astype(jnp.float32)).astype(jnp.bfloat16)
            qs[group, head * U : (head + 1) * U, 0:128] = high
            qs[group, head * U : (head + 1) * U, 128:256] = low

    my_q.wait()
    their = pl.ds(pl.multiple_of((1 - c) * T, T), T)
    remote(qraw.at[late_home, their, :], qraw.at[late_home, their, :], q_s.at[0], q_r.at[0], sibling).wait_recv()
    remote(qraw.at[1 - late_home, mine, :], qraw.at[1 - late_home, mine, :], q_s.at[1], q_r.at[1], pair).wait_recv()
    remote(
        qraw.at[1 - late_home, their, :], qraw.at[1 - late_home, their, :], q_s.at[2], q_r.at[2], pair_cross
    ).wait_recv()
    prepare(0)
    prepare(1)

    @pl.when(outer == 1)
    def _():
        hop(3, z, 0, near).wait_recv()
        start_own(3)

    hop(1, z, 0, near).wait_recv()
    to_sibling(1, z, 0).start()

    ones = jnp.ones((U, HEAD_DIM), jnp.bfloat16)

    def update(group, tile, scores, values):
        rows = pl.ds(tile * TILE, TILE)
        old = top[group, rows, :]
        new = jnp.maximum(old, jnp.max(scores, axis=1, keepdims=True))
        top[group, rows, :] = new
        factor = jnp.exp2(old - new)
        weights = jnp.exp2(scores - new[:, 0:1]).astype(jnp.bfloat16)
        term = jnp.dot(weights, values, preferred_element_type=jnp.float32)
        acc[group, rows, :] = acc[group, rows, :] * jnp.concatenate([factor, factor], axis=1) + term

    def dot_keys(group, tile, keys):
        return lax.dot_general(
            qs[group, pl.ds(tile * TILE, TILE), :],
            keys,
            (((1,), (1,)), ((), ())),
            preferred_element_type=jnp.float32,
        )

    def item_of(i):
        third = jnp.where(i == 3, 1, 0)
        first = jnp.where(i == 0, 1, 0)
        group = 1 - first - third * inner
        slot = i // 2 + 2 * third * outer
        masked = (i == 0) | (i == 4)
        return group, slot, masked

    def attend_two(k, i):
        group, slot, masked = item_of(i)
        a, b = below(k), above(k)
        keys = jnp.concatenate([kv[slot, a, 0], kv[slot, b, 0]], axis=0)
        keys = jnp.concatenate([keys, keys], axis=1)
        values = jnp.concatenate(
            [
                jnp.concatenate([kv[slot, a, 1], ones], axis=1),
                jnp.concatenate([kv[slot, b, 1], ones], axis=1),
            ],
            axis=0,
        )
        bias_a = jnp.where(masked & (z < k), NEG, 0.0).astype(jnp.float32)
        bias_b = jnp.where(masked & (z + k < Z), NEG, 0.0).astype(jnp.float32)
        column = lax.broadcasted_iota(jnp.int32, (1, 2 * U), 1)
        bias = jnp.where(column < U, bias_a, bias_b)
        for tile in range(ROWS // TILE):
            update(group, tile, dot_keys(group, tile, keys) + bias, values)

    def attend_one(zz, i, diagonal, valid):
        group, slot, masked = item_of(i)
        keys = jnp.concatenate([kv[slot, zz, 0], kv[slot, zz, 0]], axis=1)
        values = jnp.concatenate([kv[slot, zz, 1], ones], axis=1)
        column = lax.broadcasted_iota(jnp.int32, (1, U), 1)
        lift = jnp.where(masked & diagonal, 0, U)
        sink = jnp.where(masked & jnp.logical_not(valid), 4 * U, 0)
        for tile in range(ROWS // TILE):
            row = lax.broadcasted_iota(jnp.int32, (TILE, 1), 0) + tile * TILE
            row = jnp.where(row >= U, row - U, row) + lift - sink
            scores = jnp.where(column <= row, dot_keys(group, tile, keys), NEG)
            update(group, tile, scores, values)

    def attend_two_range(k, low, high):
        def body(i, carry):
            attend_two(k, i)
            return carry

        lax.fori_loop(low, high, body, 0)

    def attend_one_range(zz, low, high, diagonal, valid):
        def body(i, carry):
            attend_one(zz, i, diagonal, valid)
            return carry

        lax.fori_loop(low, high, body, 0)

    def wait_sibling(slot, k):
        from_sibling(slot, below(k), k).wait_recv()
        from_sibling(slot, above(k), k + 4).wait_recv()

    from_sibling(0, z, 0).wait_recv()
    from_sibling(1, z, 0).wait_recv()
    from_sibling(2, z, 0).wait_recv()

    @pl.when(outer == 1)
    def _():
        from_sibling(3, z, 0).wait_recv()

    attend_one_range(z, 0, 5, True, True)

    def pass_on(slot, k):
        a, b = below(k), above(k)
        hop(slot, a, k, down).wait_recv()

        @pl.when(k < 3)
        def _():
            hop(slot, a, k + 1, up).start()

        @pl.when(k == 3)
        def _():
            hop_half(slot, a, 0, 4, up).start()

        to_sibling(slot, a, k).start()
        hop(slot, b, k + 4, up).wait_recv()

        @pl.when(k < 3)
        def _():
            hop(slot, b, k + 5, down).start()

        @pl.when(k == 3)
        def _():
            hop_half(slot, b, 1, 8, down).start()

        to_sibling(slot, b, k + 4).start()

    def step(k, carry):
        pass_on(0, k)
        to_near(below(k), k).start()
        to_near(above(k), k + 4).start()

        @pl.when(k > 1)
        def _():
            wait_sibling(2, k - 1)
            attend_two_range(k - 1, 4, 5)

        @pl.when(outer == 1)
        def _():
            pass_on(3, k)

        wait_sibling(0, k)
        attend_two_range(k, 0, 2)
        pass_on(2, k)
        for msg, zz in ((k, below(k)), (k + 4, above(k))):
            hop(1, zz, msg, near).wait_recv()
            to_sibling(1, zz, msg).start()
        wait_sibling(1, k)

        @pl.when(outer == 1)
        def _():
            wait_sibling(3, k)

        attend_two_range(k, 2, 4)
        return carry

    lax.fori_loop(1, 4, step, 0)

    far = above(4)

    def pass_far(slot, near_too):
        for which, msg, source in ((0, 4, down), (1, 8, up)):
            hop_half(slot, far, which, msg, source).wait_recv()
            to_sibling_half(slot, far, which, msg).start()
            if near_too:
                to_near_half(far, which, msg).start()

    def wait_far(slot):
        from_sibling_half(slot, far, 0, 4).wait_recv()
        from_sibling_half(slot, far, 1, 8).wait_recv()

    pass_far(0, True)
    wait_sibling(2, 3)
    attend_two_range(3, 4, 5)

    @pl.when(outer == 1)
    def _():
        pass_far(3, False)

    pass_far(2, False)
    pass_far(1, False)
    for slot in (0, 1, 2):
        wait_far(slot)

    @pl.when(outer == 1)
    def _():
        wait_far(3)

    attend_one_range(far, 0, 5, False, z >= 4)

    my_cols = pl.ds(pl.multiple_of(h * 512 + c * 256, 256), 256)

    def finish(group):
        for head in range(2):
            rows = slice(head * U, (head + 1) * U)
            value = acc[group, rows, 0:128] / acc[group, rows, 128:256]
            att[group, :, head * 128 : (head + 1) * 128] = value.astype(jnp.bfloat16)

    def att_to(group, part, to, s, r):
        rows = pl.ds(pl.multiple_of(part * T, T), T)
        return remote(att.at[group, rows, :], attin.at[:, my_cols], s, r, to)

    finish(0)
    finish(1)
    away = 1 - late_home
    sends = [
        att_to(away, c, pair, att_s.at[0], att_r.at[0]),
        att_to(away, 1 - c, pair_cross, att_s.at[1], att_r.at[1]),
        att_to(late_home, 1 - c, sibling, att_s.at[2], att_r.at[2]),
    ]
    for copy in sends:
        copy.start()
    keep = pltpu.make_async_copy(att.at[late_home, mine, :], attin.at[:, my_cols], att_own)
    keep.start()
    keep.wait()
    for index, (hh, cc, source) in enumerate(((1 - h, c, pair), (1 - h, 1 - c, pair_cross), (h, 1 - c, sibling))):
        cols = pl.ds(pl.multiple_of(hh * 512 + cc * 256, 256), 256)
        remote(attin.at[:, cols], attin.at[:, cols], att_s.at[index], att_r.at[index], source).wait_recv()
    for copy in w_copies:
        copy.wait()

    def project(j, store):
        for part in range(4):
            cols = slice(part * 256, (part + 1) * 256)
            store(cols, jnp.dot(attin[...], wv[j, :, cols], preferred_element_type=jnp.float32))

    def into(ref):
        def store(cols, value):
            ref[:, cols] = value.astype(jnp.bfloat16)

        return store

    H = T // 2
    first, second = pl.ds(0, H), pl.ds(H, H)
    project(0, into(po.at[0]))
    far_up = remote(po.at[0, first, :], ro.at[0], x_s.at[0], x_r.at[0], x_up)
    far_down = remote(po.at[0, second, :], ro.at[1], x_s.at[1], x_r.at[1], x_down)
    far_up.start()
    far_down.start()
    project(1, into(pp))
    up_second = remote(pp.at[second, :], fp.at[second, :], x_s.at[2], x_r.at[2], x_up)
    up_second.start()
    project(2, into(pm))
    down_first = remote(pm.at[first, :], fm.at[first, :], x_s.at[3], x_r.at[3], x_down)
    down_first.start()
    far_up.wait_recv()
    pp[0:H, :] = (pp[0:H, :].astype(jnp.float32) + ro[0].astype(jnp.float32)).astype(jnp.bfloat16)
    up_first = remote(pp.at[first, :], fp.at[first, :], x_s.at[4], x_r.at[4], x_up)
    up_first.start()
    far_down.wait_recv()
    pm[H:T, :] = (pm[H:T, :].astype(jnp.float32) + ro[1].astype(jnp.float32)).astype(jnp.bfloat16)
    down_second = remote(pm.at[second, :], fm.at[second, :], x_s.at[5], x_r.at[5], x_down)
    down_second.start()
    project(3, into(po.at[1]))
    for copy in (up_second, down_first, up_first, down_second):
        copy.wait_recv()
    total = po[1].astype(jnp.float32) + fp[...].astype(jnp.float32) + fm[...].astype(jnp.float32)
    out_ref[...] = total.astype(jnp.bfloat16)

    for copy in (far_up, far_down, up_second, down_first, up_first, down_second, *sends, *pair_copies, *q_copies):
        copy.wait_send()

    def sent(slot):
        def whole(k, carry):
            hop(slot, z, k, up).wait_send()
            hop(slot, z, k + 4, down).wait_send()
            to_sibling(slot, z, k).wait_send()
            to_sibling(slot, z, k + 4).wait_send()
            return carry

        lax.fori_loop(1, 4, whole, 0)
        to_sibling(slot, z, 0).wait_send()
        hop_half(slot, z, 0, 4, up).wait_send()
        hop_half(slot, z, 1, 8, down).wait_send()
        to_sibling_half(slot, z, 0, 4).wait_send()
        to_sibling_half(slot, z, 1, 8).wait_send()

    sent(0)
    sent(2)

    @pl.when(outer == 1)
    def _():
        sent(3)

    @pl.when(inner == 1)
    def _():
        late_to_near().wait_send()

    def near_sent(k, carry):
        to_near(z, k).wait_send()
        to_near(z, k + 4).wait_send()
        to_sibling(1, z, k).wait_send()
        to_sibling(1, z, k + 4).wait_send()
        return carry

    lax.fori_loop(1, 4, near_sent, 0)
    to_near(z, 0).wait_send()
    to_sibling(1, z, 0).wait_send()
    to_near_half(z, 0, 4).wait_send()
    to_near_half(z, 1, 8).wait_send()
    to_sibling_half(1, z, 0, 4).wait_send()
    to_sibling_half(1, z, 1, 8).wait_send()


def local(queries, key_states, value_states, out_weight):
    bf16, f32 = jnp.bfloat16, jnp.float32
    any_spec = pl.BlockSpec(memory_space=pl.ANY)
    dma = pltpu.SemaphoreType.DMA
    return pl.pallas_call(
        kernel,
        out_shape=jax.ShapeDtypeStruct((T, 1024), bf16),
        in_specs=[any_spec] * 4,
        out_specs=pl.BlockSpec(memory_space=pltpu.VMEM),
        scratch_shapes=[
            pltpu.VMEM((4, Z, 2, U, HEAD_DIM), bf16),
            pltpu.VMEM((2, U, 256), bf16),
            pltpu.VMEM((2, ROWS, 256), bf16),
            pltpu.VMEM((2, ROWS, 256), f32),
            pltpu.VMEM((2, ROWS, HEAD_DIM), f32),
            pltpu.VMEM((2, U, 256), bf16),
            pltpu.VMEM((T, 1024), bf16),
            pltpu.VMEM((4, 1024, 1024), bf16),
            pltpu.VMEM((2, T, 1024), bf16),
            pltpu.VMEM((T, 1024), bf16),
            pltpu.VMEM((T, 1024), bf16),
            pltpu.VMEM((2, T // 2, 1024), bf16),
            pltpu.VMEM((T, 1024), bf16),
            pltpu.VMEM((T, 1024), bf16),
            dma((4, 9)), dma((4, 9)), dma((4, 9)), dma((4, 9)),
            dma((10,)), dma((2,)), dma((2,)), dma((2,)),
            dma, dma((3,)), dma((3,)), dma((4,)),
            dma((3,)), dma((3,)), dma, dma((6,)), dma((6,)),
        ],
        compiler_params=pltpu.CompilerParams(
            collective_id=0, has_side_effects=True, vmem_limit_bytes=48 << 20
        ),
    )(queries, key_states, value_states, out_weight)


def solution(mesh):
    return jax.shard_map(
        local,
        mesh=mesh,
        in_specs=(P("seq", "head"), P("seq", "head"), P("seq", "head"), P("head", None)),
        out_specs=P("seq", "head"),
        check_vma=False,
    )
```

```python
import jax
import jax.numpy as jnp
from jax import lax
from jax.experimental import pallas as pl
from jax.experimental.pallas import tpu as pltpu
from jax.sharding import PartitionSpec as P

MESH = pl.DeviceIdType.MESH
HEAD_DIM = 128
SCALE = HEAD_DIM ** -0.5 * 1.4426950408889634
NEG = -1e30
T = 192
U = 2 * T
Z = 8
ROWS = 2 * U
TILE = 256


def kernel(
    q_ref, k_ref, v_ref, w_ref, out_ref,
    kv, qraw, qs, acc, top, att, attin, wv, po, pp, pm, ro, fp, fm,
    r_sem, s_sem, sr_sem, ss_sem, ys_sem, own_sem, part_r, part_s,
    q_own, q_r, q_s, across_r, across_s, w_sem, att_r, att_s, att_own, x_r, x_s,
):
    seq, x = lax.axis_index("seq"), lax.axis_index("head")
    y, z, c = seq // 16, (seq // 2) % Z, seq % 2
    late_home = y // 2
    h = late_home
    outer = jnp.where((y == 0) | (y == 3), 1, 0)
    inner = 1 - outer
    z_up, z_down = (z + 1) % Z, (z + Z - 1) % Z
    y_near = y + 1 - 2 * (y % 2)
    y_pair = 3 - y
    xp, xm, xo = (x + 1) % 4, (x + 3) % 4, (x + 2) % 4

    def dev(yy, zz, cc, xx=None):
        return ((yy * Z + zz) * 2 + cc, x if xx is None else xx)

    up, down = dev(y, z_up, c), dev(y, z_down, c)
    near, sibling = dev(y_near, z, c), dev(y, z, 1 - c)
    pair, pair_cross = dev(y_pair, z, c), dev(y_pair, z, 1 - c)
    across = dev((y + 2) % 4, z, c)
    x_up, x_down = dev(y, z, c, xp), dev(y, z, c, xm)

    barrier = pltpu.get_barrier_semaphore()
    for other in (up, down, near, sibling, pair, pair_cross, across, x_up, x_down):
        pl.semaphore_signal(barrier, inc=1, device_id=other, device_id_type=MESH)

    mine = pl.ds(pl.multiple_of(c * T, T), T)

    def block(slot, zz):
        return kv.at[slot, zz, :, mine, :]

    def half(slot, zz, which):
        return kv.at[slot, zz, which, mine, :]

    def remote(src, dst, s, r, to):
        return pltpu.make_async_remote_copy(
            src_ref=src, dst_ref=dst, send_sem=s, recv_sem=r, device_id=to, device_id_type=MESH
        )

    own_slot = 2 * late_home
    other_slot = 2 - own_slot
    own_copies = [
        pltpu.make_async_copy(
            ref.at[:, pl.ds(pl.multiple_of(h * HEAD_DIM, HEAD_DIM), HEAD_DIM)],
            half(own_slot, z, i),
            own_sem.at[i],
        )
        for i, ref in enumerate((k_ref, v_ref))
    ]
    for copy in own_copies:
        copy.start()

    def q_cols(hh, cc):
        return q_ref.at[:, pl.ds(pl.multiple_of(hh * 512 + cc * 256, 256), 256)]

    my_q = pltpu.make_async_copy(q_cols(h, c), qraw.at[late_home, mine, :], q_own)
    my_q.start()
    pl.semaphore_wait(barrier, 9)

    pair_copies = [
        remote(
            ref.at[:, pl.ds(pl.multiple_of((1 - h) * HEAD_DIM, HEAD_DIM), HEAD_DIM)],
            half(own_slot, z, i),
            part_s.at[i],
            part_r.at[i],
            pair,
        )
        for i, ref in enumerate((k_ref, v_ref))
    ]
    for copy in pair_copies:
        copy.start()
    w_copies = [
        pltpu.make_async_copy(
            w_ref.at[:, pl.ds(pl.multiple_of(col * 1024, 1024), 1024)], wv.at[j], w_sem.at[j]
        )
        for j, col in enumerate((xo, xp, xm, x))
    ]
    def hop(slot, zz, msg, to):
        return remote(block(slot, zz), block(slot, zz), s_sem.at[slot, msg], r_sem.at[slot, msg], to)

    def hop_half(slot, zz, which, msg, to):
        return remote(
            half(slot, zz, which), half(slot, zz, which), s_sem.at[slot, msg], r_sem.at[slot, msg], to
        )

    def to_sibling(slot, zz, msg):
        return remote(block(slot, zz), block(slot, zz), ss_sem.at[slot, msg], sr_sem.at[slot, msg], sibling)

    def to_sibling_half(slot, zz, which, msg):
        return remote(
            half(slot, zz, which), half(slot, zz, which), ss_sem.at[slot, msg], sr_sem.at[slot, msg], sibling
        )

    def to_near(zz, msg):
        return remote(block(0, zz), block(1, zz), ys_sem.at[msg], r_sem.at[1, msg], near)

    def to_near_half(zz, which, msg):
        return remote(half(0, zz, which), half(1, zz, which), ys_sem.at[msg], r_sem.at[1, msg], near)

    def late_to_near():
        return remote(block(2, z), block(3, z), ys_sem.at[9], r_sem.at[3, 0], near)

    def from_sibling(slot, zz, msg):
        theirs = pl.ds(pl.multiple_of((1 - c) * T, T), T)
        ref = kv.at[slot, zz, :, theirs, :]
        return remote(ref, ref, ss_sem.at[slot, msg], sr_sem.at[slot, msg], sibling)

    def from_sibling_half(slot, zz, which, msg):
        theirs = pl.ds(pl.multiple_of((1 - c) * T, T), T)
        ref = kv.at[slot, zz, which, theirs, :]
        return remote(ref, ref, ss_sem.at[slot, msg], sr_sem.at[slot, msg], sibling)

    def below(k):
        return (z + Z - k) % Z

    def above(k):
        return (z + k) % Z

    def start_own(slot):
        hop(slot, z, 1, up).start()
        hop(slot, z, 5, down).start()
        to_sibling(slot, z, 0).start()

    def across_copy(i, ref):
        return remote(
            ref.at[:, pl.ds(pl.multiple_of((1 - h) * HEAD_DIM, HEAD_DIM), HEAD_DIM)],
            half(3, z, i),
            across_s.at[i],
            across_r.at[i],
            across,
        )

    @pl.when(y == 2)
    def _():
        for i, ref in enumerate((k_ref, v_ref)):
            across_copy(i, ref).start()

    for copy in own_copies:
        copy.wait()
    start_own(own_slot)

    @pl.when(late_home == 0)
    def _():
        to_near(z, 0).start()

    @pl.when(y == 2)
    def _():
        late_to_near().start()

    q_copies = [
        remote(q_cols(h, 1 - c), qraw.at[late_home, mine, :], q_s.at[0], q_r.at[0], sibling),
        remote(q_cols(1 - h, c), qraw.at[late_home, mine, :], q_s.at[1], q_r.at[1], pair),
        remote(q_cols(1 - h, 1 - c), qraw.at[late_home, mine, :], q_s.at[2], q_r.at[2], pair_cross),
    ]
    for copy in q_copies:
        copy.start()
    acc[...] = jnp.zeros_like(acc)
    top[...] = jnp.full_like(top, NEG)
    for i in range(2):
        remote(half(other_slot, z, i), half(other_slot, z, i), part_s.at[i], part_r.at[i], pair).wait_recv()
    start_own(other_slot)

    @pl.when(late_home == 1)
    def _():
        to_near(z, 0).start()

    for copy in w_copies:
        copy.start()

    def prepare(group):
        for head in range(2):
            value = qraw[group, :, head * 128 : (head + 1) * 128].astype(jnp.float32) * SCALE
            high = value.astype(jnp.bfloat16)
            low = (value - high.astype(jnp.float32)).astype(jnp.bfloat16)
            qs[group, head * U : (head + 1) * U, 0:128] = high
            qs[group, head * U : (head + 1) * U, 128:256] = low

    def queries_ready():
        my_q.wait()
        their = pl.ds(pl.multiple_of((1 - c) * T, T), T)
        for index, (group, rows, source) in enumerate(
            ((late_home, their, sibling), (1 - late_home, mine, pair), (1 - late_home, their, pair_cross))
        ):
            ref = qraw.at[group, rows, :]
            remote(ref, ref, q_s.at[index], q_r.at[index], source).wait_recv()
        prepare(0)
        prepare(1)

    def update(group, tile, scores, values):
        rows = pl.ds(tile * TILE, TILE)
        old = top[group, rows, :]
        new = jnp.maximum(old, jnp.max(scores, axis=1, keepdims=True))
        top[group, rows, :] = new
        factor = jnp.exp2(old - new)
        weights = jnp.exp2(scores - new[:, 0:1]).astype(jnp.bfloat16)
        term = jnp.dot(weights, values, preferred_element_type=jnp.float32)
        acc[group, rows, :] = acc[group, rows, :] * jnp.concatenate([factor, factor], axis=1) + term

    def dot_keys(group, tile, keys):
        return lax.dot_general(
            qs[group, pl.ds(tile * TILE, TILE), :],
            keys,
            (((1,), (1,)), ((), ())),
            preferred_element_type=jnp.float32,
        )

    def attend(group, pieces, fix=None):
        keys = jnp.concatenate([kv[slot, zz, 0] for slot, zz in pieces], axis=0)
        keys = jnp.concatenate([keys, keys], axis=1)
        values = jnp.concatenate([kv[slot, zz, 1] for slot, zz in pieces], axis=0)
        values = jnp.concatenate([values, jnp.ones_like(values)], axis=1)
        for tile in range(ROWS // TILE):
            scores = dot_keys(group, tile, keys)
            if fix is not None:
                scores = fix(scores, tile)
            update(group, tile, scores, values)

    def with_open(scores, open_cols, tail):
        if open_cols == 0:
            return tail
        return jnp.concatenate([scores[:, :open_cols], tail], axis=1)

    def shut(open_cols, *conditions):
        biases = [jnp.where(condition, NEG, 0.0).astype(jnp.float32) for condition in conditions]

        def fix(scores, tile):
            parts = [
                scores[:, open_cols + i * U : open_cols + (i + 1) * U] + bias for i, bias in enumerate(biases)
            ]
            return with_open(scores, open_cols, jnp.concatenate(parts, axis=1))

        return fix

    def diagonal(open_cols):
        def fix(scores, tile):
            column = lax.broadcasted_iota(jnp.int32, (1, U), 1)
            row = lax.broadcasted_iota(jnp.int32, (TILE, 1), 0) + tile * TILE
            row = jnp.where(row >= U, row - U, row)
            return with_open(scores, open_cols, jnp.where(column <= row, scores[:, open_cols:], NEG))

        return fix

    def wait_sibling(slot, k):
        from_sibling(slot, below(k), k).wait_recv()
        from_sibling(slot, above(k), k + 4).wait_recv()

    def pass_on(slot, k):
        for zz, msg, source, onward, to in ((below(k), k, down, 4, up), (above(k), k + 4, up, 8, down)):
            hop(slot, zz, msg, source).wait_recv()

            @pl.when(k < 3)
            def _(zz=zz, msg=msg, to=to):
                hop(slot, zz, msg + 1, to).start()

            @pl.when(k == 3)
            def _(zz=zz, onward=onward, to=to):
                hop_half(slot, zz, onward // 4 - 1, onward, to).start()

            to_sibling(slot, zz, msg).start()
            if slot == 0:
                to_near(zz, msg).start()

    far = above(4)

    def pass_far(slot):
        for which, msg, source in ((0, 4, down), (1, 8, up)):
            hop_half(slot, far, which, msg, source).wait_recv()
            to_sibling_half(slot, far, which, msg).start()
            if slot == 0:
                to_near_half(far, which, msg).start()

    def wait_far(slot):
        from_sibling_half(slot, far, 0, 4).wait_recv()
        from_sibling_half(slot, far, 1, 8).wait_recv()

    @pl.when(y == 3)
    def _():
        hop(3, z, 0, near).wait_recv()
        start_own(3)

    pass_on(0, 1)

    @pl.when(y == 0)
    def _():
        for i in range(2):
            remote(half(3, z, i), half(3, z, i), across_s.at[i], across_r.at[i], across).wait_recv()
        start_own(3)

    hop(1, z, 0, near).wait_recv()
    to_sibling(1, z, 0).start()
    queries_ready()
    from_sibling(0, z, 0).wait_recv()
    attend(0, [(0, z)], diagonal(0))

    @pl.when(outer == 1)
    def _():
        from_sibling(3, z, 0).wait_recv()
        attend(1, [(0, z), (3, z)])
        from_sibling(1, z, 0).wait_recv()

    @pl.when(inner == 1)
    def _():
        attend(1, [(0, z)])
        from_sibling(1, z, 0).wait_recv()
        attend(0, [(1, z)])

    pass_on(0, 2)
    from_sibling(2, z, 0).wait_recv()
    attend(1, [(1, z), (2, z)], diagonal(U))

    def step(k, carry):
        a, b = below(k), above(k)

        @pl.when(outer == 1)
        def _():
            pass_on(3, k)

        wait_sibling(0, k)
        attend(0, [(0, a), (0, b)], shut(0, z < k, z + k < Z))
        pass_on(2, k)
        for msg, zz in ((k, a), (k + 4, b)):
            hop(1, zz, msg, near).wait_recv()
            to_sibling(1, zz, msg).start()

        @pl.when(outer == 1)
        def _():
            wait_sibling(3, k)
            attend(1, [(0, a), (0, b), (3, a), (3, b)])
            wait_sibling(1, k)

        @pl.when(inner == 1)
        def _():
            attend(1, [(0, a), (0, b)])
            wait_sibling(1, k)
            attend(0, [(1, a), (1, b)])

        @pl.when(k == 1)
        def _():
            pass_on(0, 3)

        @pl.when(k == 2)
        def _():
            pass_far(0)

        @pl.when(k == 3)
        def _():
            pass_far(1)

        wait_sibling(2, k)
        attend(1, [(1, a), (1, b), (2, a), (2, b)], shut(2 * U, z < k, z + k < Z))
        return carry

    lax.fori_loop(1, 4, step, 0)

    wait_far(0)
    attend(0, [(0, far)], shut(0, z < 4))

    @pl.when(outer == 1)
    def _():
        pass_far(3)

    pass_far(2)
    wait_far(1)

    @pl.when(outer == 1)
    def _():
        wait_far(3)
        attend(1, [(0, far), (3, far)])

    @pl.when(inner == 1)
    def _():
        attend(1, [(0, far)])
        attend(0, [(1, far)])

    my_cols = pl.ds(pl.multiple_of(h * 512 + c * 256, 256), 256)
    H = T // 2

    def finish(group, part):
        for core in range(2):
            start = core * T + part * H
            for head in range(2):
                rows = slice(head * U + start, head * U + start + H)
                value = acc[group, rows, 0:128] / acc[group, rows, 128:256]
                att[group, start : start + H, head * 128 : (head + 1) * 128] = value.astype(jnp.bfloat16)

    def att_rows(core, part):
        return pl.ds(pl.multiple_of(core * T + part * H, 32), H)

    def att_to(index, group, core, part, to):
        return remote(
            att.at[group, att_rows(core, part), :],
            attin.at[pl.ds(part * H, H), my_cols],
            att_s.at[index, part],
            att_r.at[index, part],
            to,
        )

    def att_keep(part):
        return pltpu.make_async_copy(
            att.at[late_home, att_rows(c, part), :], attin.at[pl.ds(part * H, H), my_cols], att_own.at[part]
        )

    def send_attended(group, part):
        finish(group, part)

        @pl.when(late_home == group)
        def _():
            att_to(2, group, 1 - c, part, sibling).start()
            att_keep(part).start()

        @pl.when(late_home != group)
        def _():
            att_to(0, group, c, part, pair).start()
            att_to(1, group, 1 - c, part, pair_cross).start()

    def attended_ready(part):
        att_keep(part).wait()
        for index, (hh, cc, source) in enumerate(
            ((1 - h, c, pair), (1 - h, 1 - c, pair_cross), (h, 1 - c, sibling))
        ):
            cols = pl.ds(pl.multiple_of(hh * 512 + cc * 256, 256), 256)
            ref = attin.at[pl.ds(part * H, H), cols]
            remote(ref, ref, att_s.at[index, part], att_r.at[index, part], source).wait_recv()

    for part in range(2):
        send_attended(0, part)
    wait_far(2)
    attend(1, [(1, far), (2, far)], shut(U, z < 4))
    for part in range(2):
        send_attended(1, part)
    for copy in w_copies:
        copy.wait()

    def project(j, part, ref):
        rows = slice(part * H, (part + 1) * H)
        for piece in range(4):
            cols = slice(piece * 256, (piece + 1) * 256)
            value = jnp.dot(attin[rows, :], wv[j, :, cols], preferred_element_type=jnp.float32)
            ref[rows, cols] = value.astype(jnp.bfloat16)

    first, second = pl.ds(0, H), pl.ds(H, H)
    far_up = remote(po.at[0, first, :], ro.at[0], x_s.at[0], x_r.at[0], x_up)
    far_down = remote(po.at[0, second, :], ro.at[1], x_s.at[1], x_r.at[1], x_down)
    up_second = remote(pp.at[second, :], fp.at[second, :], x_s.at[2], x_r.at[2], x_up)
    down_first = remote(pm.at[first, :], fm.at[first, :], x_s.at[3], x_r.at[3], x_down)
    up_first = remote(pp.at[first, :], fp.at[first, :], x_s.at[4], x_r.at[4], x_up)
    down_second = remote(pm.at[second, :], fm.at[second, :], x_s.at[5], x_r.at[5], x_down)
    attended_ready(0)
    project(0, 0, po.at[0])
    far_up.start()
    project(2, 0, pm)
    down_first.start()
    attended_ready(1)
    project(0, 1, po.at[0])
    far_down.start()
    project(1, 1, pp)
    up_second.start()
    project(1, 0, pp)
    far_up.wait_recv()
    pp[0:H, :] = (pp[0:H, :].astype(jnp.float32) + ro[0].astype(jnp.float32)).astype(jnp.bfloat16)
    up_first.start()
    project(2, 1, pm)
    far_down.wait_recv()
    pm[H:T, :] = (pm[H:T, :].astype(jnp.float32) + ro[1].astype(jnp.float32)).astype(jnp.bfloat16)
    down_second.start()
    project(3, 0, po.at[1])
    project(3, 1, po.at[1])

    def total(part):
        rows = slice(part * H, (part + 1) * H)
        value = po[1, rows, :].astype(jnp.float32) + fp[rows, :].astype(jnp.float32)
        out_ref[rows, :] = (value + fm[rows, :].astype(jnp.float32)).astype(jnp.bfloat16)

    down_first.wait_recv()
    up_first.wait_recv()
    total(0)
    up_second.wait_recv()
    down_second.wait_recv()
    total(1)

    for copy in (far_up, far_down, up_second, down_first, up_first, down_second, *pair_copies, *q_copies):
        copy.wait_send()

    for part in range(2):
        att_to(0, 0, c, part, pair).wait_send()
        att_to(1, 0, 1 - c, part, pair_cross).wait_send()
        att_to(2, 0, 1 - c, part, sibling).wait_send()

    def sent(slot):
        def whole(k, carry):
            hop(slot, z, k, up).wait_send()
            hop(slot, z, k + 4, down).wait_send()
            to_sibling(slot, z, k).wait_send()
            to_sibling(slot, z, k + 4).wait_send()
            return carry

        lax.fori_loop(1, 4, whole, 0)
        to_sibling(slot, z, 0).wait_send()
        hop_half(slot, z, 0, 4, up).wait_send()
        hop_half(slot, z, 1, 8, down).wait_send()
        to_sibling_half(slot, z, 0, 4).wait_send()
        to_sibling_half(slot, z, 1, 8).wait_send()

    sent(0)
    sent(2)

    @pl.when(outer == 1)
    def _():
        sent(3)

    @pl.when(y == 2)
    def _():
        late_to_near().wait_send()
        for i, ref in enumerate((k_ref, v_ref)):
            across_copy(i, ref).wait_send()

    def near_sent(k, carry):
        to_near(z, k).wait_send()
        to_near(z, k + 4).wait_send()
        to_sibling(1, z, k).wait_send()
        to_sibling(1, z, k + 4).wait_send()
        return carry

    lax.fori_loop(1, 4, near_sent, 0)
    to_near(z, 0).wait_send()
    to_sibling(1, z, 0).wait_send()
    to_near_half(z, 0, 4).wait_send()
    to_near_half(z, 1, 8).wait_send()
    to_sibling_half(1, z, 0, 4).wait_send()
    to_sibling_half(1, z, 1, 8).wait_send()


def local(queries, key_states, value_states, out_weight):
    bf16, f32 = jnp.bfloat16, jnp.float32
    any_spec = pl.BlockSpec(memory_space=pl.ANY)
    dma = pltpu.SemaphoreType.DMA
    return pl.pallas_call(
        kernel,
        out_shape=jax.ShapeDtypeStruct((T, 1024), bf16),
        in_specs=[any_spec] * 4,
        out_specs=pl.BlockSpec(memory_space=pltpu.VMEM),
        scratch_shapes=[
            pltpu.VMEM((4, Z, 2, U, HEAD_DIM), bf16),
            pltpu.VMEM((2, U, 256), bf16),
            pltpu.VMEM((2, ROWS, 256), bf16),
            pltpu.VMEM((2, ROWS, 256), f32),
            pltpu.VMEM((2, ROWS, HEAD_DIM), f32),
            pltpu.VMEM((2, U, 256), bf16),
            pltpu.VMEM((T, 1024), bf16),
            pltpu.VMEM((4, 1024, 1024), bf16),
            pltpu.VMEM((2, T, 1024), bf16),
            pltpu.VMEM((T, 1024), bf16),
            pltpu.VMEM((T, 1024), bf16),
            pltpu.VMEM((2, T // 2, 1024), bf16),
            pltpu.VMEM((T, 1024), bf16),
            pltpu.VMEM((T, 1024), bf16),
            dma((4, 9)), dma((4, 9)), dma((4, 9)), dma((4, 9)),
            dma((10,)), dma((2,)), dma((2,)), dma((2,)),
            dma, dma((3,)), dma((3,)), dma((2,)), dma((2,)), dma((4,)),
            dma((3, 2)), dma((3, 2)), dma((2,)), dma((6,)), dma((6,)),
        ],
        compiler_params=pltpu.CompilerParams(
            collective_id=0, has_side_effects=True, vmem_limit_bytes=60 << 20
        ),
    )(queries, key_states, value_states, out_weight)


def solution(mesh):
    return jax.shard_map(
        local,
        mesh=mesh,
        in_specs=(P("seq", "head"), P("seq", "head"), P("seq", "head"), P("head", None)),
        out_specs=P("seq", "head"),
        check_vma=False,
    )
```

```python
import jax
import jax.numpy as jnp
from jax import lax
from jax.experimental import pallas as pl
from jax.experimental.pallas import tpu as pltpu
from jax.sharding import PartitionSpec as P

MESH = pl.DeviceIdType.MESH
HEAD_DIM = 128
SCALE = HEAD_DIM ** -0.5 * 1.4426950408889634
NEG = -1e30
T = 192
U = 2 * T
Z = 8
ROWS = 2 * U
TILE = 256


def kernel(
    q_ref, k_ref, v_ref, w_ref, out_ref,
    kv, qraw, qs, acc, top, att, attin, wv, po, pp, pm, ro, fp, fm,
    r_sem, s_sem, sr_sem, ss_sem, ys_sem, own_sem, part_r, part_s,
    q_own, q_r, q_s, across_r, across_s, w_sem, att_r, att_s, att_own, x_r, x_s,
):
    seq, x = lax.axis_index("seq"), lax.axis_index("head")
    y, z, c = seq // 16, (seq // 2) % Z, seq % 2
    late_home = y // 2
    h = late_home
    outer = jnp.where((y == 0) | (y == 3), 1, 0)
    inner = 1 - outer
    z_up, z_down = (z + 1) % Z, (z + Z - 1) % Z
    y_near = y + 1 - 2 * (y % 2)
    y_pair = 3 - y
    xp, xm, xo = (x + 1) % 4, (x + 3) % 4, (x + 2) % 4

    def dev(yy, zz, cc, xx=None):
        return ((yy * Z + zz) * 2 + cc, x if xx is None else xx)

    up, down = dev(y, z_up, c), dev(y, z_down, c)
    near, sibling = dev(y_near, z, c), dev(y, z, 1 - c)
    pair, pair_cross = dev(y_pair, z, c), dev(y_pair, z, 1 - c)
    across = dev((y + 2) % 4, z, c)
    x_up, x_down = dev(y, z, c, xp), dev(y, z, c, xm)

    barrier = pltpu.get_barrier_semaphore()
    for other in (up, down, near, sibling, pair, pair_cross, across, x_up, x_down):
        pl.semaphore_signal(barrier, inc=1, device_id=other, device_id_type=MESH)

    mine = pl.ds(pl.multiple_of(c * T, T), T)

    def block(slot, zz):
        return kv.at[slot, zz, :, mine, :]

    def half(slot, zz, which):
        return kv.at[slot, zz, which, mine, :]

    def remote(src, dst, s, r, to):
        return pltpu.make_async_remote_copy(
            src_ref=src, dst_ref=dst, send_sem=s, recv_sem=r, device_id=to, device_id_type=MESH
        )

    own_slot = 2 * late_home
    other_slot = 2 - own_slot
    own_copies = [
        pltpu.make_async_copy(
            ref.at[:, pl.ds(pl.multiple_of(h * HEAD_DIM, HEAD_DIM), HEAD_DIM)],
            half(own_slot, z, i),
            own_sem.at[i],
        )
        for i, ref in enumerate((k_ref, v_ref))
    ]
    for copy in own_copies:
        copy.start()

    def q_cols(hh, cc):
        return q_ref.at[:, pl.ds(pl.multiple_of(hh * 512 + cc * 256, 256), 256)]

    my_q = pltpu.make_async_copy(q_cols(h, c), qraw.at[late_home, mine, :], q_own)
    my_q.start()
    pl.semaphore_wait(barrier, 9)

    pair_copies = [
        remote(
            ref.at[:, pl.ds(pl.multiple_of((1 - h) * HEAD_DIM, HEAD_DIM), HEAD_DIM)],
            half(own_slot, z, i),
            part_s.at[i],
            part_r.at[i],
            pair,
        )
        for i, ref in enumerate((k_ref, v_ref))
    ]
    for copy in pair_copies:
        copy.start()
    w_copies = [
        pltpu.make_async_copy(
            w_ref.at[:, pl.ds(pl.multiple_of(col * 1024, 1024), 1024)], wv.at[j], w_sem.at[j]
        )
        for j, col in enumerate((xo, xp, xm, x))
    ]
    def hop(slot, zz, msg, to):
        return remote(block(slot, zz), block(slot, zz), s_sem.at[slot, msg], r_sem.at[slot, msg], to)

    def hop_half(slot, zz, which, msg, to):
        return remote(
            half(slot, zz, which), half(slot, zz, which), s_sem.at[slot, msg], r_sem.at[slot, msg], to
        )

    def to_sibling(slot, zz, msg):
        return remote(block(slot, zz), block(slot, zz), ss_sem.at[slot, msg], sr_sem.at[slot, msg], sibling)

    def to_sibling_half(slot, zz, which, msg):
        return remote(
            half(slot, zz, which), half(slot, zz, which), ss_sem.at[slot, msg], sr_sem.at[slot, msg], sibling
        )

    def to_near(zz, msg):
        return remote(block(0, zz), block(1, zz), ys_sem.at[msg], r_sem.at[1, msg], near)

    def to_near_half(zz, which, msg):
        return remote(half(0, zz, which), half(1, zz, which), ys_sem.at[msg], r_sem.at[1, msg], near)

    def late_to_near():
        return remote(block(2, z), block(3, z), ys_sem.at[9], r_sem.at[3, 0], near)

    def from_sibling(slot, zz, msg):
        theirs = pl.ds(pl.multiple_of((1 - c) * T, T), T)
        ref = kv.at[slot, zz, :, theirs, :]
        return remote(ref, ref, ss_sem.at[slot, msg], sr_sem.at[slot, msg], sibling)

    def from_sibling_half(slot, zz, which, msg):
        theirs = pl.ds(pl.multiple_of((1 - c) * T, T), T)
        ref = kv.at[slot, zz, which, theirs, :]
        return remote(ref, ref, ss_sem.at[slot, msg], sr_sem.at[slot, msg], sibling)

    def below(k):
        return (z + Z - k) % Z

    def above(k):
        return (z + k) % Z

    def start_own(slot):
        hop(slot, z, 1, up).start()
        hop(slot, z, 5, down).start()
        to_sibling(slot, z, 0).start()

    def across_copy(i, ref):
        return remote(
            ref.at[:, pl.ds(pl.multiple_of((1 - h) * HEAD_DIM, HEAD_DIM), HEAD_DIM)],
            half(3, z, i),
            across_s.at[i],
            across_r.at[i],
            across,
        )

    @pl.when(y == 2)
    def _():
        for i, ref in enumerate((k_ref, v_ref)):
            across_copy(i, ref).start()

    for copy in own_copies:
        copy.wait()
    start_own(own_slot)

    @pl.when(late_home == 0)
    def _():
        to_near(z, 0).start()

    @pl.when(y == 2)
    def _():
        late_to_near().start()

    q_copies = [
        remote(q_cols(h, 1 - c), qraw.at[late_home, mine, :], q_s.at[0], q_r.at[0], sibling),
        remote(q_cols(1 - h, c), qraw.at[late_home, mine, :], q_s.at[1], q_r.at[1], pair),
        remote(q_cols(1 - h, 1 - c), qraw.at[late_home, mine, :], q_s.at[2], q_r.at[2], pair_cross),
    ]
    for copy in q_copies:
        copy.start()
    acc[...] = jnp.zeros_like(acc)
    top[...] = jnp.full_like(top, NEG)
    for i in range(2):
        remote(half(other_slot, z, i), half(other_slot, z, i), part_s.at[i], part_r.at[i], pair).wait_recv()
    start_own(other_slot)

    @pl.when(late_home == 1)
    def _():
        to_near(z, 0).start()

    for copy in w_copies:
        copy.start()

    def prepare(group):
        for head in range(2):
            value = qraw[group, :, head * 128 : (head + 1) * 128].astype(jnp.float32) * SCALE
            high = value.astype(jnp.bfloat16)
            low = (value - high.astype(jnp.float32)).astype(jnp.bfloat16)
            qs[group, head * U : (head + 1) * U, 0:128] = high
            qs[group, head * U : (head + 1) * U, 128:256] = low

    def queries_ready():
        my_q.wait()
        their = pl.ds(pl.multiple_of((1 - c) * T, T), T)
        for index, (group, rows, source) in enumerate(
            ((late_home, their, sibling), (1 - late_home, mine, pair), (1 - late_home, their, pair_cross))
        ):
            ref = qraw.at[group, rows, :]
            remote(ref, ref, q_s.at[index], q_r.at[index], source).wait_recv()
        prepare(0)
        prepare(1)

    def update(group, tile, scores, values):
        rows = pl.ds(tile * TILE, TILE)
        old = top[group, rows, :]
        new = jnp.maximum(old, jnp.max(scores, axis=1, keepdims=True))
        top[group, rows, :] = new
        factor = jnp.exp2(old - new)
        weights = jnp.exp2(scores - new[:, 0:1]).astype(jnp.bfloat16)
        term = jnp.dot(weights, values, preferred_element_type=jnp.float32)
        acc[group, rows, :] = acc[group, rows, :] * jnp.concatenate([factor, factor], axis=1) + term

    def dot_keys(group, tile, keys):
        return lax.dot_general(
            qs[group, pl.ds(tile * TILE, TILE), :],
            keys,
            (((1,), (1,)), ((), ())),
            preferred_element_type=jnp.float32,
        )

    def attend(group, pieces, fix=None):
        keys = jnp.concatenate([kv[slot, zz, 0] for slot, zz in pieces], axis=0)
        keys = jnp.concatenate([keys, keys], axis=1)
        values = jnp.concatenate([kv[slot, zz, 1] for slot, zz in pieces], axis=0)
        values = jnp.concatenate([values, jnp.ones_like(values)], axis=1)
        for tile in range(ROWS // TILE):
            scores = dot_keys(group, tile, keys)
            if fix is not None:
                scores = fix(scores, tile)
            update(group, tile, scores, values)

    def with_open(scores, open_cols, tail):
        if open_cols == 0:
            return tail
        return jnp.concatenate([scores[:, :open_cols], tail], axis=1)

    def shut(open_cols, *conditions):
        biases = [jnp.where(condition, NEG, 0.0).astype(jnp.float32) for condition in conditions]

        def fix(scores, tile):
            parts = [
                scores[:, open_cols + i * U : open_cols + (i + 1) * U] + bias for i, bias in enumerate(biases)
            ]
            return with_open(scores, open_cols, jnp.concatenate(parts, axis=1))

        return fix

    def diagonal(open_cols):
        def fix(scores, tile):
            column = lax.broadcasted_iota(jnp.int32, (1, U), 1)
            row = lax.broadcasted_iota(jnp.int32, (TILE, 1), 0) + tile * TILE
            row = jnp.where(row >= U, row - U, row)
            return with_open(scores, open_cols, jnp.where(column <= row, scores[:, open_cols:], NEG))

        return fix

    def wait_sibling(slot, k):
        from_sibling(slot, below(k), k).wait_recv()
        from_sibling(slot, above(k), k + 4).wait_recv()

    def pass_on(slot, k):
        for zz, msg, source, onward, to in ((below(k), k, down, 4, up), (above(k), k + 4, up, 8, down)):
            hop(slot, zz, msg, source).wait_recv()

            @pl.when(k < 3)
            def _(zz=zz, msg=msg, to=to):
                hop(slot, zz, msg + 1, to).start()

            @pl.when(k == 3)
            def _(zz=zz, onward=onward, to=to):
                hop_half(slot, zz, onward // 4 - 1, onward, to).start()

            to_sibling(slot, zz, msg).start()
            if slot == 0:
                to_near(zz, msg).start()

    far = above(4)

    def pass_far(slot):
        for which, msg, source in ((0, 4, down), (1, 8, up)):
            hop_half(slot, far, which, msg, source).wait_recv()
            to_sibling_half(slot, far, which, msg).start()
            if slot == 0:
                to_near_half(far, which, msg).start()

    def wait_far(slot):
        from_sibling_half(slot, far, 0, 4).wait_recv()
        from_sibling_half(slot, far, 1, 8).wait_recv()

    @pl.when(y == 3)
    def _():
        hop(3, z, 0, near).wait_recv()
        start_own(3)

    pass_on(0, 1)

    @pl.when(y == 0)
    def _():
        for i in range(2):
            remote(half(3, z, i), half(3, z, i), across_s.at[i], across_r.at[i], across).wait_recv()
        start_own(3)

    hop(1, z, 0, near).wait_recv()
    to_sibling(1, z, 0).start()
    queries_ready()
    from_sibling(0, z, 0).wait_recv()
    attend(0, [(0, z)], diagonal(0))

    @pl.when(outer == 1)
    def _():
        from_sibling(3, z, 0).wait_recv()
        attend(1, [(0, z), (3, z)])
        from_sibling(1, z, 0).wait_recv()

    @pl.when(inner == 1)
    def _():
        attend(1, [(0, z)])
        from_sibling(1, z, 0).wait_recv()
        attend(0, [(1, z)])

    pass_on(0, 2)
    from_sibling(2, z, 0).wait_recv()
    attend(1, [(1, z), (2, z)], diagonal(U))

    def step(k, carry):
        a, b = below(k), above(k)

        @pl.when(outer == 1)
        def _():
            pass_on(3, k)

        wait_sibling(0, k)
        attend(0, [(0, a), (0, b)], shut(0, z < k, z + k < Z))
        pass_on(2, k)
        for msg, zz in ((k, a), (k + 4, b)):
            hop(1, zz, msg, near).wait_recv()
            to_sibling(1, zz, msg).start()

        @pl.when(outer == 1)
        def _():
            wait_sibling(3, k)
            attend(1, [(0, a), (0, b), (3, a), (3, b)])
            wait_sibling(1, k)

        @pl.when(inner == 1)
        def _():
            attend(1, [(0, a), (0, b)])
            wait_sibling(1, k)
            attend(0, [(1, a), (1, b)])

        @pl.when(k == 1)
        def _():
            pass_on(0, 3)

        @pl.when(k == 2)
        def _():
            pass_far(0)

        @pl.when(k == 3)
        def _():
            pass_far(1)

        wait_sibling(2, k)
        attend(1, [(1, a), (1, b), (2, a), (2, b)], shut(2 * U, z < k, z + k < Z))
        return carry

    lax.fori_loop(1, 4, step, 0)

    wait_far(0)
    attend(0, [(0, far)], shut(0, z < 4))

    @pl.when(outer == 1)
    def _():
        pass_far(3)

    pass_far(2)
    wait_far(1)

    @pl.when(outer == 1)
    def _():
        wait_far(3)
        attend(1, [(0, far), (3, far)])

    @pl.when(inner == 1)
    def _():
        attend(1, [(0, far)])
        attend(0, [(1, far)])

    my_cols = pl.ds(pl.multiple_of(h * 512 + c * 256, 256), 256)
    H = T // 2

    def finish(group, part):
        for core in range(2):
            start = core * T + part * H
            for head in range(2):
                rows = slice(head * U + start, head * U + start + H)
                value = acc[group, rows, 0:128] / acc[group, rows, 128:256]
                att[group, start : start + H, head * 128 : (head + 1) * 128] = value.astype(jnp.bfloat16)

    def att_rows(core, part):
        return pl.ds(pl.multiple_of(core * T + part * H, 32), H)

    def att_to(index, group, core, part, to):
        return remote(
            att.at[group, att_rows(core, part), :],
            attin.at[pl.ds(part * H, H), my_cols],
            att_s.at[index, part],
            att_r.at[index, part],
            to,
        )

    def att_keep(part):
        return pltpu.make_async_copy(
            att.at[late_home, att_rows(c, part), :], attin.at[pl.ds(part * H, H), my_cols], att_own.at[part]
        )

    def send_attended(group, part):
        finish(group, part)

        @pl.when(late_home == group)
        def _():
            att_to(2, group, 1 - c, part, sibling).start()
            att_keep(part).start()

        @pl.when(late_home != group)
        def _():
            att_to(0, group, c, part, pair).start()
            att_to(1, group, 1 - c, part, pair_cross).start()

    def attended_ready(part):
        att_keep(part).wait()
        for index, (hh, cc, source) in enumerate(
            ((1 - h, c, pair), (1 - h, 1 - c, pair_cross), (h, 1 - c, sibling))
        ):
            cols = pl.ds(pl.multiple_of(hh * 512 + cc * 256, 256), 256)
            ref = attin.at[pl.ds(part * H, H), cols]
            remote(ref, ref, att_s.at[index, part], att_r.at[index, part], source).wait_recv()

    for part in range(2):
        send_attended(0, part)
    wait_far(2)
    attend(1, [(1, far), (2, far)], shut(U, z < 4))
    for part in range(2):
        send_attended(1, part)
    for copy in w_copies:
        copy.wait()

    def project(j, part, ref):
        rows = slice(part * H, (part + 1) * H)
        for piece in range(4):
            cols = slice(piece * 256, (piece + 1) * 256)
            value = jnp.dot(attin[rows, :], wv[j, :, cols], preferred_element_type=jnp.float32)
            ref[rows, cols] = value.astype(jnp.bfloat16)

    left, right = pl.ds(0, 512), pl.ds(512, 512)

    def x_copies(part):
        rows = pl.ds(part * H, H)

        def copy(index, src, dst, to):
            return remote(src, dst, x_s.at[index, part], x_r.at[index, part], to)

        return (
            copy(0, po.at[0, rows, left], ro.at[0, rows, :], x_up),
            copy(1, po.at[0, rows, right], ro.at[1, rows, :], x_down),
            copy(2, pp.at[rows, right], fp.at[rows, right], x_up),
            copy(3, pm.at[rows, left], fm.at[rows, left], x_down),
            copy(4, pp.at[rows, left], fp.at[rows, left], x_up),
            copy(5, pm.at[rows, right], fm.at[rows, right], x_down),
        )

    shares = [x_copies(part) for part in range(2)]
    for part in range(2):
        far_up, far_down, up_plain, down_plain, up_sum, down_sum = shares[part]
        attended_ready(part)
        project(0, part, po.at[0])
        far_up.start()
        far_down.start()
        project(1, part, pp)
        up_plain.start()
        project(2, part, pm)
        down_plain.start()
    for part in range(2):
        far_up, far_down, up_plain, down_plain, up_sum, down_sum = shares[part]
        rows = slice(part * H, (part + 1) * H)
        far_up.wait_recv()
        value = pp[rows, 0:512].astype(jnp.float32) + ro[0, rows, :].astype(jnp.float32)
        pp[rows, 0:512] = value.astype(jnp.bfloat16)
        up_sum.start()
        far_down.wait_recv()
        value = pm[rows, 512:1024].astype(jnp.float32) + ro[1, rows, :].astype(jnp.float32)
        pm[rows, 512:1024] = value.astype(jnp.bfloat16)
        down_sum.start()
    project(3, 0, po.at[1])
    project(3, 1, po.at[1])

    def total(part):
        rows = slice(part * H, (part + 1) * H)
        value = po[1, rows, :].astype(jnp.float32) + fp[rows, :].astype(jnp.float32)
        out_ref[rows, :] = (value + fm[rows, :].astype(jnp.float32)).astype(jnp.bfloat16)

    for part in range(2):
        for copy in shares[part][2:]:
            copy.wait_recv()
        total(part)

    for copy in (*shares[0], *shares[1], *pair_copies, *q_copies):
        copy.wait_send()

    for part in range(2):
        att_to(0, 0, c, part, pair).wait_send()
        att_to(1, 0, 1 - c, part, pair_cross).wait_send()
        att_to(2, 0, 1 - c, part, sibling).wait_send()

    def sent(slot):
        def whole(k, carry):
            hop(slot, z, k, up).wait_send()
            hop(slot, z, k + 4, down).wait_send()
            to_sibling(slot, z, k).wait_send()
            to_sibling(slot, z, k + 4).wait_send()
            return carry

        lax.fori_loop(1, 4, whole, 0)
        to_sibling(slot, z, 0).wait_send()
        hop_half(slot, z, 0, 4, up).wait_send()
        hop_half(slot, z, 1, 8, down).wait_send()
        to_sibling_half(slot, z, 0, 4).wait_send()
        to_sibling_half(slot, z, 1, 8).wait_send()

    sent(0)
    sent(2)

    @pl.when(outer == 1)
    def _():
        sent(3)

    @pl.when(y == 2)
    def _():
        late_to_near().wait_send()
        for i, ref in enumerate((k_ref, v_ref)):
            across_copy(i, ref).wait_send()

    def near_sent(k, carry):
        to_near(z, k).wait_send()
        to_near(z, k + 4).wait_send()
        to_sibling(1, z, k).wait_send()
        to_sibling(1, z, k + 4).wait_send()
        return carry

    lax.fori_loop(1, 4, near_sent, 0)
    to_near(z, 0).wait_send()
    to_sibling(1, z, 0).wait_send()
    to_near_half(z, 0, 4).wait_send()
    to_near_half(z, 1, 8).wait_send()
    to_sibling_half(1, z, 0, 4).wait_send()
    to_sibling_half(1, z, 1, 8).wait_send()


def local(queries, key_states, value_states, out_weight):
    bf16, f32 = jnp.bfloat16, jnp.float32
    any_spec = pl.BlockSpec(memory_space=pl.ANY)
    dma = pltpu.SemaphoreType.DMA
    return pl.pallas_call(
        kernel,
        out_shape=jax.ShapeDtypeStruct((T, 1024), bf16),
        in_specs=[any_spec] * 4,
        out_specs=pl.BlockSpec(memory_space=pltpu.VMEM),
        scratch_shapes=[
            pltpu.VMEM((4, Z, 2, U, HEAD_DIM), bf16),
            pltpu.VMEM((2, U, 256), bf16),
            pltpu.VMEM((2, ROWS, 256), bf16),
            pltpu.VMEM((2, ROWS, 256), f32),
            pltpu.VMEM((2, ROWS, HEAD_DIM), f32),
            pltpu.VMEM((2, U, 256), bf16),
            pltpu.VMEM((T, 1024), bf16),
            pltpu.VMEM((4, 1024, 1024), bf16),
            pltpu.VMEM((2, T, 1024), bf16),
            pltpu.VMEM((T, 1024), bf16),
            pltpu.VMEM((T, 1024), bf16),
            pltpu.VMEM((2, T, 512), bf16),
            pltpu.VMEM((T, 1024), bf16),
            pltpu.VMEM((T, 1024), bf16),
            dma((4, 9)), dma((4, 9)), dma((4, 9)), dma((4, 9)),
            dma((10,)), dma((2,)), dma((2,)), dma((2,)),
            dma, dma((3,)), dma((3,)), dma((2,)), dma((2,)), dma((4,)),
            dma((3, 2)), dma((3, 2)), dma((2,)), dma((6, 2)), dma((6, 2)),
        ],
        compiler_params=pltpu.CompilerParams(
            collective_id=0, has_side_effects=True, vmem_limit_bytes=60 << 20
        ),
    )(queries, key_states, value_states, out_weight)


def solution(mesh):
    return jax.shard_map(
        local,
        mesh=mesh,
        in_specs=(P("seq", "head"), P("seq", "head"), P("seq", "head"), P("head", None)),
        out_specs=P("seq", "head"),
        check_vma=False,
    )
```

```python
import jax
import jax.numpy as jnp
from jax import lax
from jax.experimental import pallas as pl
from jax.experimental.pallas import tpu as pltpu
from jax.sharding import PartitionSpec as P

MESH = pl.DeviceIdType.MESH
HEAD_DIM = 128
SCALE = HEAD_DIM ** -0.5 * 1.4426950408889634
NEG = -1e30
T = 192
U = 2 * T
Z = 8
ROWS = 2 * U
TILE = 256


def kernel(
    q_ref, k_ref, v_ref, w_ref, share_ref, fp, fm,
    kv, qraw, qs, acc, top, att, attin, wv, po, pp, pm, ro,
    r_sem, s_sem, sr_sem, ss_sem, ys_sem, own_sem, part_r, part_s,
    q_own, q_r, q_s, across_r, across_s, w_sem, att_r, att_s, att_own, x_r, x_s, share_sem,
):
    seq, x = lax.axis_index("seq"), lax.axis_index("head")
    y, z, c = seq // 16, (seq // 2) % Z, seq % 2
    late_home = y // 2
    h = late_home
    outer = jnp.where((y == 0) | (y == 3), 1, 0)
    inner = 1 - outer
    z_up, z_down = (z + 1) % Z, (z + Z - 1) % Z
    y_near = y + 1 - 2 * (y % 2)
    y_pair = 3 - y
    xp, xm, xo = (x + 1) % 4, (x + 3) % 4, (x + 2) % 4

    def dev(yy, zz, cc, xx=None):
        return ((yy * Z + zz) * 2 + cc, x if xx is None else xx)

    up, down = dev(y, z_up, c), dev(y, z_down, c)
    near, sibling = dev(y_near, z, c), dev(y, z, 1 - c)
    pair, pair_cross = dev(y_pair, z, c), dev(y_pair, z, 1 - c)
    across = dev((y + 2) % 4, z, c)
    x_up, x_down = dev(y, z, c, xp), dev(y, z, c, xm)

    barrier = pltpu.get_barrier_semaphore()
    for other in (up, down, near, sibling, pair, pair_cross, across, x_up, x_down):
        pl.semaphore_signal(barrier, inc=1, device_id=other, device_id_type=MESH)

    mine = pl.ds(pl.multiple_of(c * T, T), T)

    def block(slot, zz):
        return kv.at[slot, zz, :, mine, :]

    def half(slot, zz, which):
        return kv.at[slot, zz, which, mine, :]

    def remote(src, dst, s, r, to):
        return pltpu.make_async_remote_copy(
            src_ref=src, dst_ref=dst, send_sem=s, recv_sem=r, device_id=to, device_id_type=MESH
        )

    own_slot = 2 * late_home
    other_slot = 2 - own_slot
    own_copies = [
        pltpu.make_async_copy(
            ref.at[:, pl.ds(pl.multiple_of(h * HEAD_DIM, HEAD_DIM), HEAD_DIM)],
            half(own_slot, z, i),
            own_sem.at[i],
        )
        for i, ref in enumerate((k_ref, v_ref))
    ]
    for copy in own_copies:
        copy.start()

    def q_cols(hh, cc):
        return q_ref.at[:, pl.ds(pl.multiple_of(hh * 512 + cc * 256, 256), 256)]

    my_q = pltpu.make_async_copy(q_cols(h, c), qraw.at[late_home, mine, :], q_own)
    my_q.start()
    pl.semaphore_wait(barrier, 9)

    pair_copies = [
        remote(
            ref.at[:, pl.ds(pl.multiple_of((1 - h) * HEAD_DIM, HEAD_DIM), HEAD_DIM)],
            half(own_slot, z, i),
            part_s.at[i],
            part_r.at[i],
            pair,
        )
        for i, ref in enumerate((k_ref, v_ref))
    ]
    for copy in pair_copies:
        copy.start()
    w_copies = [
        pltpu.make_async_copy(
            w_ref.at[:, pl.ds(pl.multiple_of(col * 1024, 1024), 1024)], wv.at[j], w_sem.at[j]
        )
        for j, col in enumerate((xo, xp, xm, x))
    ]
    def hop(slot, zz, msg, to):
        return remote(block(slot, zz), block(slot, zz), s_sem.at[slot, msg], r_sem.at[slot, msg], to)

    def hop_half(slot, zz, which, msg, to):
        return remote(
            half(slot, zz, which), half(slot, zz, which), s_sem.at[slot, msg], r_sem.at[slot, msg], to
        )

    def to_sibling(slot, zz, msg):
        return remote(block(slot, zz), block(slot, zz), ss_sem.at[slot, msg], sr_sem.at[slot, msg], sibling)

    def to_sibling_half(slot, zz, which, msg):
        return remote(
            half(slot, zz, which), half(slot, zz, which), ss_sem.at[slot, msg], sr_sem.at[slot, msg], sibling
        )

    def to_near(zz, msg):
        return remote(block(0, zz), block(1, zz), ys_sem.at[msg], r_sem.at[1, msg], near)

    def to_near_half(zz, which, msg):
        return remote(half(0, zz, which), half(1, zz, which), ys_sem.at[msg], r_sem.at[1, msg], near)

    def late_to_near():
        return remote(block(2, z), block(3, z), ys_sem.at[9], r_sem.at[3, 0], near)

    def from_sibling(slot, zz, msg):
        theirs = pl.ds(pl.multiple_of((1 - c) * T, T), T)
        ref = kv.at[slot, zz, :, theirs, :]
        return remote(ref, ref, ss_sem.at[slot, msg], sr_sem.at[slot, msg], sibling)

    def from_sibling_half(slot, zz, which, msg):
        theirs = pl.ds(pl.multiple_of((1 - c) * T, T), T)
        ref = kv.at[slot, zz, which, theirs, :]
        return remote(ref, ref, ss_sem.at[slot, msg], sr_sem.at[slot, msg], sibling)

    def below(k):
        return (z + Z - k) % Z

    def above(k):
        return (z + k) % Z

    def start_own(slot):
        hop(slot, z, 1, up).start()
        hop(slot, z, 5, down).start()
        to_sibling(slot, z, 0).start()

    def across_copy(i, ref):
        return remote(
            ref.at[:, pl.ds(pl.multiple_of((1 - h) * HEAD_DIM, HEAD_DIM), HEAD_DIM)],
            half(3, z, i),
            across_s.at[i],
            across_r.at[i],
            across,
        )

    @pl.when(y == 2)
    def _():
        for i, ref in enumerate((k_ref, v_ref)):
            across_copy(i, ref).start()

    for copy in own_copies:
        copy.wait()
    start_own(own_slot)

    @pl.when(late_home == 0)
    def _():
        to_near(z, 0).start()

    @pl.when(y == 2)
    def _():
        late_to_near().start()

    q_copies = [
        remote(q_cols(h, 1 - c), qraw.at[late_home, mine, :], q_s.at[0], q_r.at[0], sibling),
        remote(q_cols(1 - h, c), qraw.at[late_home, mine, :], q_s.at[1], q_r.at[1], pair),
        remote(q_cols(1 - h, 1 - c), qraw.at[late_home, mine, :], q_s.at[2], q_r.at[2], pair_cross),
    ]
    for copy in q_copies:
        copy.start()
    acc[...] = jnp.zeros_like(acc)
    top[...] = jnp.full_like(top, NEG)
    for i in range(2):
        remote(half(other_slot, z, i), half(other_slot, z, i), part_s.at[i], part_r.at[i], pair).wait_recv()
    start_own(other_slot)

    @pl.when(late_home == 1)
    def _():
        to_near(z, 0).start()

    for copy in w_copies:
        copy.start()

    def prepare(group):
        for head in range(2):
            value = qraw[group, :, head * 128 : (head + 1) * 128].astype(jnp.float32) * SCALE
            high = value.astype(jnp.bfloat16)
            low = (value - high.astype(jnp.float32)).astype(jnp.bfloat16)
            qs[group, head * U : (head + 1) * U, 0:128] = high
            qs[group, head * U : (head + 1) * U, 128:256] = low

    def queries_ready():
        my_q.wait()
        their = pl.ds(pl.multiple_of((1 - c) * T, T), T)
        for index, (group, rows, source) in enumerate(
            ((late_home, their, sibling), (1 - late_home, mine, pair), (1 - late_home, their, pair_cross))
        ):
            ref = qraw.at[group, rows, :]
            remote(ref, ref, q_s.at[index], q_r.at[index], source).wait_recv()
        prepare(0)
        prepare(1)

    def update(group, tile, scores, values):
        rows = pl.ds(tile * TILE, TILE)
        old = top[group, rows, :]
        new = jnp.maximum(old, jnp.max(scores, axis=1, keepdims=True))
        top[group, rows, :] = new
        factor = jnp.exp2(old - new)
        weights = jnp.exp2(scores - new[:, 0:1]).astype(jnp.bfloat16)
        term = jnp.dot(weights, values, preferred_element_type=jnp.float32)
        acc[group, rows, :] = acc[group, rows, :] * jnp.concatenate([factor, factor], axis=1) + term

    def dot_keys(group, tile, keys):
        return lax.dot_general(
            qs[group, pl.ds(tile * TILE, TILE), :],
            keys,
            (((1,), (1,)), ((), ())),
            preferred_element_type=jnp.float32,
        )

    def attend(group, pieces, fix=None):
        keys = jnp.concatenate([kv[slot, zz, 0] for slot, zz in pieces], axis=0)
        keys = jnp.concatenate([keys, keys], axis=1)
        values = jnp.concatenate([kv[slot, zz, 1] for slot, zz in pieces], axis=0)
        values = jnp.concatenate([values, jnp.ones_like(values)], axis=1)
        for tile in range(ROWS // TILE):
            scores = dot_keys(group, tile, keys)
            if fix is not None:
                scores = fix(scores, tile)
            update(group, tile, scores, values)

    def with_open(scores, open_cols, tail):
        if open_cols == 0:
            return tail
        return jnp.concatenate([scores[:, :open_cols], tail], axis=1)

    def shut(open_cols, *conditions):
        biases = [jnp.where(condition, NEG, 0.0).astype(jnp.float32) for condition in conditions]

        def fix(scores, tile):
            parts = [
                scores[:, open_cols + i * U : open_cols + (i + 1) * U] + bias for i, bias in enumerate(biases)
            ]
            return with_open(scores, open_cols, jnp.concatenate(parts, axis=1))

        return fix

    def diagonal(open_cols):
        def fix(scores, tile):
            column = lax.broadcasted_iota(jnp.int32, (1, U), 1)
            row = lax.broadcasted_iota(jnp.int32, (TILE, 1), 0) + tile * TILE
            row = jnp.where(row >= U, row - U, row)
            return with_open(scores, open_cols, jnp.where(column <= row, scores[:, open_cols:], NEG))

        return fix

    def wait_sibling(slot, k):
        from_sibling(slot, below(k), k).wait_recv()
        from_sibling(slot, above(k), k + 4).wait_recv()

    def pass_on(slot, k):
        for zz, msg, source, onward, to in ((below(k), k, down, 4, up), (above(k), k + 4, up, 8, down)):
            hop(slot, zz, msg, source).wait_recv()

            @pl.when(k < 3)
            def _(zz=zz, msg=msg, to=to):
                hop(slot, zz, msg + 1, to).start()

            @pl.when(k == 3)
            def _(zz=zz, onward=onward, to=to):
                hop_half(slot, zz, onward // 4 - 1, onward, to).start()

            to_sibling(slot, zz, msg).start()
            if slot == 0:
                to_near(zz, msg).start()

    far = above(4)

    def pass_far(slot):
        for which, msg, source in ((0, 4, down), (1, 8, up)):
            hop_half(slot, far, which, msg, source).wait_recv()
            to_sibling_half(slot, far, which, msg).start()
            if slot == 0:
                to_near_half(far, which, msg).start()

    def wait_far(slot):
        from_sibling_half(slot, far, 0, 4).wait_recv()
        from_sibling_half(slot, far, 1, 8).wait_recv()

    @pl.when(y == 3)
    def _():
        hop(3, z, 0, near).wait_recv()
        start_own(3)

    pass_on(0, 1)

    @pl.when(y == 0)
    def _():
        for i in range(2):
            remote(half(3, z, i), half(3, z, i), across_s.at[i], across_r.at[i], across).wait_recv()
        start_own(3)

    hop(1, z, 0, near).wait_recv()
    to_sibling(1, z, 0).start()
    queries_ready()
    from_sibling(0, z, 0).wait_recv()
    attend(0, [(0, z)], diagonal(0))

    @pl.when(outer == 1)
    def _():
        from_sibling(3, z, 0).wait_recv()
        attend(1, [(0, z), (3, z)])
        from_sibling(1, z, 0).wait_recv()

    @pl.when(inner == 1)
    def _():
        attend(1, [(0, z)])
        from_sibling(1, z, 0).wait_recv()
        attend(0, [(1, z)])

    pass_on(0, 2)
    from_sibling(2, z, 0).wait_recv()
    attend(1, [(1, z), (2, z)], diagonal(U))

    def step(k, carry):
        a, b = below(k), above(k)

        @pl.when(outer == 1)
        def _():
            pass_on(3, k)

        wait_sibling(0, k)
        attend(0, [(0, a), (0, b)], shut(0, z < k, z + k < Z))
        pass_on(2, k)
        for msg, zz in ((k, a), (k + 4, b)):
            hop(1, zz, msg, near).wait_recv()
            to_sibling(1, zz, msg).start()

        @pl.when(outer == 1)
        def _():
            wait_sibling(3, k)
            attend(1, [(0, a), (0, b), (3, a), (3, b)])
            wait_sibling(1, k)

        @pl.when(inner == 1)
        def _():
            attend(1, [(0, a), (0, b)])
            wait_sibling(1, k)
            attend(0, [(1, a), (1, b)])

        @pl.when(k == 1)
        def _():
            pass_on(0, 3)

        @pl.when(k == 2)
        def _():
            pass_far(0)

        @pl.when(k == 3)
        def _():
            pass_far(1)

        wait_sibling(2, k)
        attend(1, [(1, a), (1, b), (2, a), (2, b)], shut(2 * U, z < k, z + k < Z))
        return carry

    lax.fori_loop(1, 4, step, 0)

    wait_far(0)
    attend(0, [(0, far)], shut(0, z < 4))

    @pl.when(outer == 1)
    def _():
        pass_far(3)

    pass_far(2)
    wait_far(1)

    @pl.when(outer == 1)
    def _():
        wait_far(3)
        attend(1, [(0, far), (3, far)])

    @pl.when(inner == 1)
    def _():
        attend(1, [(0, far)])
        attend(0, [(1, far)])

    my_cols = pl.ds(pl.multiple_of(h * 512 + c * 256, 256), 256)
    H = T // 2

    def finish(group, part):
        for core in range(2):
            start = core * T + part * H
            for head in range(2):
                rows = slice(head * U + start, head * U + start + H)
                value = acc[group, rows, 0:128] / acc[group, rows, 128:256]
                att[group, start : start + H, head * 128 : (head + 1) * 128] = value.astype(jnp.bfloat16)

    def att_rows(core, part):
        return pl.ds(pl.multiple_of(core * T + part * H, 32), H)

    def att_to(index, group, core, part, to):
        return remote(
            att.at[group, att_rows(core, part), :],
            attin.at[pl.ds(part * H, H), my_cols],
            att_s.at[index, part],
            att_r.at[index, part],
            to,
        )

    def att_keep(part):
        return pltpu.make_async_copy(
            att.at[late_home, att_rows(c, part), :], attin.at[pl.ds(part * H, H), my_cols], att_own.at[part]
        )

    def send_attended(group, part):
        finish(group, part)

        @pl.when(late_home == group)
        def _():
            att_to(2, group, 1 - c, part, sibling).start()
            att_keep(part).start()

        @pl.when(late_home != group)
        def _():
            att_to(0, group, c, part, pair).start()
            att_to(1, group, 1 - c, part, pair_cross).start()

    def attended_ready(part):
        att_keep(part).wait()
        for index, (hh, cc, source) in enumerate(
            ((1 - h, c, pair), (1 - h, 1 - c, pair_cross), (h, 1 - c, sibling))
        ):
            cols = pl.ds(pl.multiple_of(hh * 512 + cc * 256, 256), 256)
            ref = attin.at[pl.ds(part * H, H), cols]
            remote(ref, ref, att_s.at[index, part], att_r.at[index, part], source).wait_recv()

    for part in range(2):
        send_attended(0, part)
    wait_far(2)
    attend(1, [(1, far), (2, far)], shut(U, z < 4))
    for part in range(2):
        send_attended(1, part)
    for copy in w_copies:
        copy.wait()

    def project(j, part, ref):
        rows = slice(part * H, (part + 1) * H)
        for piece in range(4):
            cols = slice(piece * 256, (piece + 1) * 256)
            value = jnp.dot(attin[rows, :], wv[j, :, cols], preferred_element_type=jnp.float32)
            ref[rows, cols] = value.astype(jnp.bfloat16)

    left, right = pl.ds(0, 512), pl.ds(512, 512)

    def x_copies(part):
        rows = pl.ds(part * H, H)

        def copy(index, src, dst, to):
            return remote(src, dst, x_s.at[index, part], x_r.at[index, part], to)

        return (
            copy(0, po.at[0, rows, left], ro.at[0, rows, :], x_up),
            copy(1, po.at[0, rows, right], ro.at[1, rows, :], x_down),
            copy(2, pp.at[rows, right], fp.at[rows, right], x_up),
            copy(3, pm.at[rows, left], fm.at[rows, left], x_down),
            copy(4, pp.at[rows, left], fp.at[rows, left], x_up),
            copy(5, pm.at[rows, right], fm.at[rows, right], x_down),
        )

    shares = [x_copies(part) for part in range(2)]
    for part in range(2):
        far_up, far_down, up_plain, down_plain, up_sum, down_sum = shares[part]
        attended_ready(part)
        project(0, part, po.at[0])
        far_up.start()
        far_down.start()
        project(1, part, pp)
        up_plain.start()
        project(2, part, pm)
        down_plain.start()
    for part in range(2):
        far_up, far_down, up_plain, down_plain, up_sum, down_sum = shares[part]
        rows = slice(part * H, (part + 1) * H)
        far_up.wait_recv()
        value = pp[rows, 0:512].astype(jnp.float32) + ro[0, rows, :].astype(jnp.float32)
        pp[rows, 0:512] = value.astype(jnp.bfloat16)
        up_sum.start()
        far_down.wait_recv()
        value = pm[rows, 512:1024].astype(jnp.float32) + ro[1, rows, :].astype(jnp.float32)
        pm[rows, 512:1024] = value.astype(jnp.bfloat16)
        down_sum.start()
    project(3, 0, po.at[1])
    project(3, 1, po.at[1])
    own_share = pltpu.make_async_copy(po.at[1], share_ref, share_sem)
    own_share.start()
    for part in range(2):
        for copy in shares[part][2:]:
            copy.wait_recv()
    own_share.wait()

    for copy in (*shares[0], *shares[1], *pair_copies, *q_copies):
        copy.wait_send()

    for part in range(2):
        att_to(0, 0, c, part, pair).wait_send()
        att_to(1, 0, 1 - c, part, pair_cross).wait_send()
        att_to(2, 0, 1 - c, part, sibling).wait_send()

    def sent(slot):
        def whole(k, carry):
            hop(slot, z, k, up).wait_send()
            hop(slot, z, k + 4, down).wait_send()
            to_sibling(slot, z, k).wait_send()
            to_sibling(slot, z, k + 4).wait_send()
            return carry

        lax.fori_loop(1, 4, whole, 0)
        to_sibling(slot, z, 0).wait_send()
        hop_half(slot, z, 0, 4, up).wait_send()
        hop_half(slot, z, 1, 8, down).wait_send()
        to_sibling_half(slot, z, 0, 4).wait_send()
        to_sibling_half(slot, z, 1, 8).wait_send()

    sent(0)
    sent(2)

    @pl.when(outer == 1)
    def _():
        sent(3)

    @pl.when(y == 2)
    def _():
        late_to_near().wait_send()
        for i, ref in enumerate((k_ref, v_ref)):
            across_copy(i, ref).wait_send()

    def near_sent(k, carry):
        to_near(z, k).wait_send()
        to_near(z, k + 4).wait_send()
        to_sibling(1, z, k).wait_send()
        to_sibling(1, z, k + 4).wait_send()
        return carry

    lax.fori_loop(1, 4, near_sent, 0)
    to_near(z, 0).wait_send()
    to_sibling(1, z, 0).wait_send()
    to_near_half(z, 0, 4).wait_send()
    to_near_half(z, 1, 8).wait_send()
    to_sibling_half(1, z, 0, 4).wait_send()
    to_sibling_half(1, z, 1, 8).wait_send()


def local(queries, key_states, value_states, out_weight):
    bf16, f32 = jnp.bfloat16, jnp.float32
    any_spec = pl.BlockSpec(memory_space=pl.ANY)
    dma = pltpu.SemaphoreType.DMA
    share, from_below, from_above = pl.pallas_call(
        kernel,
        out_shape=[jax.ShapeDtypeStruct((T, 1024), bf16)] * 3,
        in_specs=[any_spec] * 4,
        out_specs=[any_spec] * 3,
        scratch_shapes=[
            pltpu.VMEM((4, Z, 2, U, HEAD_DIM), bf16),
            pltpu.VMEM((2, U, 256), bf16),
            pltpu.VMEM((2, ROWS, 256), bf16),
            pltpu.VMEM((2, ROWS, 256), f32),
            pltpu.VMEM((2, ROWS, HEAD_DIM), f32),
            pltpu.VMEM((2, U, 256), bf16),
            pltpu.VMEM((T, 1024), bf16),
            pltpu.VMEM((4, 1024, 1024), bf16),
            pltpu.VMEM((2, T, 1024), bf16),
            pltpu.VMEM((T, 1024), bf16),
            pltpu.VMEM((T, 1024), bf16),
            pltpu.VMEM((2, T, 512), bf16),
            dma((4, 9)), dma((4, 9)), dma((4, 9)), dma((4, 9)),
            dma((10,)), dma((2,)), dma((2,)), dma((2,)),
            dma, dma((3,)), dma((3,)), dma((2,)), dma((2,)), dma((4,)),
            dma((3, 2)), dma((3, 2)), dma((2,)), dma((6, 2)), dma((6, 2)), dma,
        ],
        compiler_params=pltpu.CompilerParams(
            collective_id=0, has_side_effects=True, vmem_limit_bytes=60 << 20
        ),
    )(queries, key_states, value_states, out_weight)
    return (share.astype(f32) + from_below.astype(f32) + from_above.astype(f32)).astype(bf16)


def solution(mesh):
    return jax.shard_map(
        local,
        mesh=mesh,
        in_specs=(P("seq", "head"), P("seq", "head"), P("seq", "head"), P("head", None)),
        out_specs=P("seq", "head"),
        check_vma=False,
    )
```

```python
import jax
import jax.numpy as jnp
from jax import lax
from jax.experimental import pallas as pl
from jax.experimental.pallas import tpu as pltpu
from jax.sharding import PartitionSpec as P

MESH = pl.DeviceIdType.MESH
HEAD_DIM = 128
SCALE = HEAD_DIM ** -0.5 * 1.4426950408889634
NEG = -1e30
T = 192
U = 2 * T
Z = 8
ROWS = 2 * U
TILE = 256


def kernel(
    q_ref, k_ref, v_ref, w_ref, share_ref, fp, fm,
    kv, qraw, qs, acc, top, att, attin, wv, po, pp, pm, ro,
    r_sem, s_sem, sr_sem, ss_sem, ys_sem, own_sem, part_r, part_s,
    q_own, q_r, q_s, across_r, across_s, w_sem, att_r, att_s, att_own, x_r, x_s, share_sem,
):
    seq, x = lax.axis_index("seq"), lax.axis_index("head")
    y, z, c = seq // 16, (seq // 2) % Z, seq % 2
    late_home = y // 2
    h = late_home
    outer = jnp.where((y == 0) | (y == 3), 1, 0)
    inner = 1 - outer
    z_up, z_down = (z + 1) % Z, (z + Z - 1) % Z
    y_near = y + 1 - 2 * (y % 2)
    y_pair = 3 - y
    xp, xm, xo = (x + 1) % 4, (x + 3) % 4, (x + 2) % 4

    def dev(yy, zz, cc, xx=None):
        return ((yy * Z + zz) * 2 + cc, x if xx is None else xx)

    up, down = dev(y, z_up, c), dev(y, z_down, c)
    near, sibling = dev(y_near, z, c), dev(y, z, 1 - c)
    pair, pair_cross = dev(y_pair, z, c), dev(y_pair, z, 1 - c)
    across = dev((y + 2) % 4, z, c)
    x_up, x_down = dev(y, z, c, xp), dev(y, z, c, xm)

    barrier = pltpu.get_barrier_semaphore()
    for other in (up, down, near, sibling, pair, pair_cross, across, x_up, x_down):
        pl.semaphore_signal(barrier, inc=1, device_id=other, device_id_type=MESH)

    mine = pl.ds(pl.multiple_of(c * T, T), T)

    def block(slot, zz):
        return kv.at[slot, zz, :, mine, :]

    def half(slot, zz, which):
        return kv.at[slot, zz, which, mine, :]

    def remote(src, dst, s, r, to):
        return pltpu.make_async_remote_copy(
            src_ref=src, dst_ref=dst, send_sem=s, recv_sem=r, device_id=to, device_id_type=MESH
        )

    own_slot = 2 * late_home
    other_slot = 2 - own_slot
    own_copies = [
        pltpu.make_async_copy(
            ref.at[:, pl.ds(pl.multiple_of(h * HEAD_DIM, HEAD_DIM), HEAD_DIM)],
            half(own_slot, z, i),
            own_sem.at[i],
        )
        for i, ref in enumerate((k_ref, v_ref))
    ]
    for copy in own_copies:
        copy.start()

    def q_cols(hh, cc):
        return q_ref.at[:, pl.ds(pl.multiple_of(hh * 512 + cc * 256, 256), 256)]

    my_q = pltpu.make_async_copy(q_cols(h, c), qraw.at[late_home, mine, :], q_own)
    my_q.start()
    pl.semaphore_wait(barrier, 9)

    pair_copies = [
        remote(
            ref.at[:, pl.ds(pl.multiple_of((1 - h) * HEAD_DIM, HEAD_DIM), HEAD_DIM)],
            half(own_slot, z, i),
            part_s.at[i],
            part_r.at[i],
            pair,
        )
        for i, ref in enumerate((k_ref, v_ref))
    ]
    for copy in pair_copies:
        copy.start()
    w_copies = [
        pltpu.make_async_copy(
            w_ref.at[:, pl.ds(pl.multiple_of(col * 1024, 1024), 1024)], wv.at[j], w_sem.at[j]
        )
        for j, col in enumerate((xo, xp, xm, x))
    ]
    def hop(slot, zz, msg, to):
        return remote(block(slot, zz), block(slot, zz), s_sem.at[slot, msg], r_sem.at[slot, msg], to)

    def hop_half(slot, zz, which, msg, to):
        return remote(
            half(slot, zz, which), half(slot, zz, which), s_sem.at[slot, msg], r_sem.at[slot, msg], to
        )

    def to_sibling(slot, zz, msg):
        return remote(block(slot, zz), block(slot, zz), ss_sem.at[slot, msg], sr_sem.at[slot, msg], sibling)

    def to_sibling_half(slot, zz, which, msg):
        return remote(
            half(slot, zz, which), half(slot, zz, which), ss_sem.at[slot, msg], sr_sem.at[slot, msg], sibling
        )

    def to_near(zz, msg):
        return remote(block(0, zz), block(1, zz), ys_sem.at[msg], r_sem.at[1, msg], near)

    def to_near_half(zz, which, msg):
        return remote(half(0, zz, which), half(1, zz, which), ys_sem.at[msg], r_sem.at[1, msg], near)

    def late_to_near():
        return remote(block(2, z), block(3, z), ys_sem.at[9], r_sem.at[3, 0], near)

    def from_sibling(slot, zz, msg):
        theirs = pl.ds(pl.multiple_of((1 - c) * T, T), T)
        ref = kv.at[slot, zz, :, theirs, :]
        return remote(ref, ref, ss_sem.at[slot, msg], sr_sem.at[slot, msg], sibling)

    def from_sibling_half(slot, zz, which, msg):
        theirs = pl.ds(pl.multiple_of((1 - c) * T, T), T)
        ref = kv.at[slot, zz, which, theirs, :]
        return remote(ref, ref, ss_sem.at[slot, msg], sr_sem.at[slot, msg], sibling)

    def below(k):
        return (z + Z - k) % Z

    def above(k):
        return (z + k) % Z

    def start_own(slot):
        hop(slot, z, 1, up).start()
        hop(slot, z, 5, down).start()
        to_sibling(slot, z, 0).start()

    def across_copy(i, ref):
        return remote(
            ref.at[:, pl.ds(pl.multiple_of((1 - h) * HEAD_DIM, HEAD_DIM), HEAD_DIM)],
            half(3, z, i),
            across_s.at[i],
            across_r.at[i],
            across,
        )

    @pl.when(y == 2)
    def _():
        for i, ref in enumerate((k_ref, v_ref)):
            across_copy(i, ref).start()

    for copy in own_copies:
        copy.wait()
    start_own(own_slot)

    @pl.when(late_home == 0)
    def _():
        to_near(z, 0).start()

    @pl.when(y == 2)
    def _():
        late_to_near().start()

    q_copies = [
        remote(q_cols(h, 1 - c), qraw.at[late_home, mine, :], q_s.at[0], q_r.at[0], sibling),
        remote(q_cols(1 - h, c), qraw.at[late_home, mine, :], q_s.at[1], q_r.at[1], pair),
        remote(q_cols(1 - h, 1 - c), qraw.at[late_home, mine, :], q_s.at[2], q_r.at[2], pair_cross),
    ]
    for copy in q_copies:
        copy.start()
    acc[...] = jnp.zeros_like(acc)
    top[...] = jnp.full_like(top, NEG)
    for i in range(2):
        remote(half(other_slot, z, i), half(other_slot, z, i), part_s.at[i], part_r.at[i], pair).wait_recv()
    start_own(other_slot)

    @pl.when(late_home == 1)
    def _():
        to_near(z, 0).start()

    for copy in w_copies:
        copy.start()

    def prepare(group):
        for head in range(2):
            value = qraw[group, :, head * 128 : (head + 1) * 128].astype(jnp.float32) * SCALE
            high = value.astype(jnp.bfloat16)
            low = (value - high.astype(jnp.float32)).astype(jnp.bfloat16)
            qs[group, head * U : (head + 1) * U, 0:128] = high
            qs[group, head * U : (head + 1) * U, 128:256] = low

    def queries_ready():
        their = pl.ds(pl.multiple_of((1 - c) * T, T), T)
        my_q.wait()
        ref = qraw.at[late_home, their, :]
        remote(ref, ref, q_s.at[0], q_r.at[0], sibling).wait_recv()
        prepare(late_home)
        for index, rows, source in ((1, mine, pair), (2, their, pair_cross)):
            ref = qraw.at[1 - late_home, rows, :]
            remote(ref, ref, q_s.at[index], q_r.at[index], source).wait_recv()
        prepare(1 - late_home)

    def update(group, tile, scores, values):
        rows = pl.ds(tile * TILE, TILE)
        old = top[group, rows, :]
        new = jnp.maximum(old, jnp.max(scores, axis=1, keepdims=True))
        top[group, rows, :] = new
        factor = jnp.exp2(old - new)
        weights = jnp.exp2(scores - new[:, 0:1]).astype(jnp.bfloat16)
        term = jnp.dot(weights, values, preferred_element_type=jnp.float32)
        acc[group, rows, :] = acc[group, rows, :] * jnp.concatenate([factor, factor], axis=1) + term

    def dot_keys(group, tile, keys):
        return lax.dot_general(
            qs[group, pl.ds(tile * TILE, TILE), :],
            keys,
            (((1,), (1,)), ((), ())),
            preferred_element_type=jnp.float32,
        )

    def attend(group, pieces, fix=None):
        keys = jnp.concatenate([kv[slot, zz, 0] for slot, zz in pieces], axis=0)
        keys = jnp.concatenate([keys, keys], axis=1)
        values = jnp.concatenate([kv[slot, zz, 1] for slot, zz in pieces], axis=0)
        values = jnp.concatenate([values, jnp.ones_like(values)], axis=1)
        for tile in range(ROWS // TILE):
            scores = dot_keys(group, tile, keys)
            if fix is not None:
                scores = fix(scores, tile)
            update(group, tile, scores, values)

    def with_open(scores, open_cols, tail):
        if open_cols == 0:
            return tail
        return jnp.concatenate([scores[:, :open_cols], tail], axis=1)

    def shut(open_cols, *conditions):
        biases = [jnp.where(condition, NEG, 0.0).astype(jnp.float32) for condition in conditions]

        def fix(scores, tile):
            parts = [
                scores[:, open_cols + i * U : open_cols + (i + 1) * U] + bias for i, bias in enumerate(biases)
            ]
            return with_open(scores, open_cols, jnp.concatenate(parts, axis=1))

        return fix

    def diagonal(open_cols):
        def fix(scores, tile):
            column = lax.broadcasted_iota(jnp.int32, (1, U), 1)
            row = lax.broadcasted_iota(jnp.int32, (TILE, 1), 0) + tile * TILE
            row = jnp.where(row >= U, row - U, row)
            return with_open(scores, open_cols, jnp.where(column <= row, scores[:, open_cols:], NEG))

        return fix

    def wait_sibling(slot, k):
        from_sibling(slot, below(k), k).wait_recv()
        from_sibling(slot, above(k), k + 4).wait_recv()

    def pass_on(slot, k):
        for zz, msg, source, onward, to in ((below(k), k, down, 4, up), (above(k), k + 4, up, 8, down)):
            hop(slot, zz, msg, source).wait_recv()

            @pl.when(k < 3)
            def _(zz=zz, msg=msg, to=to):
                hop(slot, zz, msg + 1, to).start()

            @pl.when(k == 3)
            def _(zz=zz, onward=onward, to=to):
                hop_half(slot, zz, onward // 4 - 1, onward, to).start()

            to_sibling(slot, zz, msg).start()
            if slot == 0:
                to_near(zz, msg).start()

    far = above(4)

    def pass_far(slot):
        for which, msg, source in ((0, 4, down), (1, 8, up)):
            hop_half(slot, far, which, msg, source).wait_recv()
            to_sibling_half(slot, far, which, msg).start()
            if slot == 0:
                to_near_half(far, which, msg).start()

    def wait_far(slot):
        from_sibling_half(slot, far, 0, 4).wait_recv()
        from_sibling_half(slot, far, 1, 8).wait_recv()

    @pl.when(y == 3)
    def _():
        hop(3, z, 0, near).wait_recv()
        start_own(3)

    pass_on(0, 1)

    @pl.when(y == 0)
    def _():
        for i in range(2):
            remote(half(3, z, i), half(3, z, i), across_s.at[i], across_r.at[i], across).wait_recv()
        start_own(3)

    hop(1, z, 0, near).wait_recv()
    to_sibling(1, z, 0).start()
    queries_ready()
    from_sibling(0, z, 0).wait_recv()
    attend(0, [(0, z)], diagonal(0))

    @pl.when(outer == 1)
    def _():
        from_sibling(3, z, 0).wait_recv()
        attend(1, [(0, z), (3, z)])
        from_sibling(1, z, 0).wait_recv()

    @pl.when(inner == 1)
    def _():
        attend(1, [(0, z)])
        from_sibling(1, z, 0).wait_recv()
        attend(0, [(1, z)])

    pass_on(0, 2)
    from_sibling(2, z, 0).wait_recv()
    attend(1, [(1, z), (2, z)], diagonal(U))

    def step(k, carry):
        a, b = below(k), above(k)

        @pl.when(outer == 1)
        def _():
            pass_on(3, k)

        wait_sibling(0, k)
        attend(0, [(0, a), (0, b)], shut(0, z < k, z + k < Z))
        pass_on(2, k)
        for msg, zz in ((k, a), (k + 4, b)):
            hop(1, zz, msg, near).wait_recv()
            to_sibling(1, zz, msg).start()

        @pl.when(outer == 1)
        def _():
            wait_sibling(3, k)
            attend(1, [(0, a), (0, b), (3, a), (3, b)])
            wait_sibling(1, k)

        @pl.when(inner == 1)
        def _():
            attend(1, [(0, a), (0, b)])
            wait_sibling(1, k)
            attend(0, [(1, a), (1, b)])

        @pl.when(k == 1)
        def _():
            pass_on(0, 3)

        @pl.when(k == 2)
        def _():
            pass_far(0)

        @pl.when(k == 3)
        def _():
            pass_far(1)

        wait_sibling(2, k)
        attend(1, [(1, a), (1, b), (2, a), (2, b)], shut(2 * U, z < k, z + k < Z))
        return carry

    lax.fori_loop(1, 4, step, 0)

    wait_far(0)
    attend(0, [(0, far)], shut(0, z < 4))

    @pl.when(outer == 1)
    def _():
        pass_far(3)

    pass_far(2)
    wait_far(1)

    @pl.when(outer == 1)
    def _():
        wait_far(3)
        attend(1, [(0, far), (3, far)])

    @pl.when(inner == 1)
    def _():
        attend(1, [(0, far)])
        attend(0, [(1, far)])

    my_cols = pl.ds(pl.multiple_of(h * 512 + c * 256, 256), 256)
    H = T // 2

    def finish(group, part):
        for core in range(2):
            start = core * T + part * H
            for head in range(2):
                rows = slice(head * U + start, head * U + start + H)
                value = acc[group, rows, 0:128] / acc[group, rows, 128:256]
                att[group, start : start + H, head * 128 : (head + 1) * 128] = value.astype(jnp.bfloat16)

    def att_rows(core, part):
        return pl.ds(pl.multiple_of(core * T + part * H, 32), H)

    def att_to(index, group, core, part, to):
        return remote(
            att.at[group, att_rows(core, part), :],
            attin.at[pl.ds(part * H, H), my_cols],
            att_s.at[index, part],
            att_r.at[index, part],
            to,
        )

    def att_keep(part):
        return pltpu.make_async_copy(
            att.at[late_home, att_rows(c, part), :], attin.at[pl.ds(part * H, H), my_cols], att_own.at[part]
        )

    def send_attended(group, part):
        finish(group, part)

        @pl.when(late_home == group)
        def _():
            att_to(2, group, 1 - c, part, sibling).start()
            att_keep(part).start()

        @pl.when(late_home != group)
        def _():
            att_to(0, group, c, part, pair).start()
            att_to(1, group, 1 - c, part, pair_cross).start()

    def attended_ready(part):
        att_keep(part).wait()
        for index, (hh, cc, source) in enumerate(
            ((1 - h, c, pair), (1 - h, 1 - c, pair_cross), (h, 1 - c, sibling))
        ):
            cols = pl.ds(pl.multiple_of(hh * 512 + cc * 256, 256), 256)
            ref = attin.at[pl.ds(part * H, H), cols]
            remote(ref, ref, att_s.at[index, part], att_r.at[index, part], source).wait_recv()

    for part in range(2):
        send_attended(0, part)
    wait_far(2)
    attend(1, [(1, far), (2, far)], shut(U, z < 4))
    for part in range(2):
        send_attended(1, part)
    for copy in w_copies:
        copy.wait()

    def project(j, part, ref):
        rows = slice(part * H, (part + 1) * H)
        for piece in range(4):
            cols = slice(piece * 256, (piece + 1) * 256)
            value = jnp.dot(attin[rows, :], wv[j, :, cols], preferred_element_type=jnp.float32)
            ref[rows, cols] = value.astype(jnp.bfloat16)

    left, right = pl.ds(0, 512), pl.ds(512, 512)

    def x_copies(part):
        rows = pl.ds(part * H, H)

        def copy(index, src, dst, to):
            return remote(src, dst, x_s.at[index, part], x_r.at[index, part], to)

        return (
            copy(0, po.at[0, rows, left], ro.at[0, rows, :], x_up),
            copy(1, po.at[0, rows, right], ro.at[1, rows, :], x_down),
            copy(2, pp.at[rows, right], fp.at[rows, right], x_up),
            copy(3, pm.at[rows, left], fm.at[rows, left], x_down),
            copy(4, pp.at[rows, left], fp.at[rows, left], x_up),
            copy(5, pm.at[rows, right], fm.at[rows, right], x_down),
        )

    shares = [x_copies(part) for part in range(2)]
    for part in range(2):
        far_up, far_down, up_plain, down_plain, up_sum, down_sum = shares[part]
        attended_ready(part)
        project(0, part, po.at[0])
        far_up.start()
        far_down.start()
        project(1, part, pp)
        up_plain.start()
        project(2, part, pm)
        down_plain.start()
    for part in range(2):
        far_up, far_down, up_plain, down_plain, up_sum, down_sum = shares[part]
        rows = slice(part * H, (part + 1) * H)
        far_up.wait_recv()
        value = pp[rows, 0:512].astype(jnp.float32) + ro[0, rows, :].astype(jnp.float32)
        pp[rows, 0:512] = value.astype(jnp.bfloat16)
        up_sum.start()
        far_down.wait_recv()
        value = pm[rows, 512:1024].astype(jnp.float32) + ro[1, rows, :].astype(jnp.float32)
        pm[rows, 512:1024] = value.astype(jnp.bfloat16)
        down_sum.start()
    project(3, 0, po.at[1])
    project(3, 1, po.at[1])
    own_share = pltpu.make_async_copy(po.at[1], share_ref, share_sem)
    own_share.start()
    for part in range(2):
        for copy in shares[part][2:]:
            copy.wait_recv()
    own_share.wait()

    for copy in (*shares[0], *shares[1], *pair_copies, *q_copies):
        copy.wait_send()

    for part in range(2):
        att_to(0, 0, c, part, pair).wait_send()
        att_to(1, 0, 1 - c, part, pair_cross).wait_send()
        att_to(2, 0, 1 - c, part, sibling).wait_send()

    def sent(slot):
        def whole(k, carry):
            hop(slot, z, k, up).wait_send()
            hop(slot, z, k + 4, down).wait_send()
            to_sibling(slot, z, k).wait_send()
            to_sibling(slot, z, k + 4).wait_send()
            return carry

        lax.fori_loop(1, 4, whole, 0)
        to_sibling(slot, z, 0).wait_send()
        hop_half(slot, z, 0, 4, up).wait_send()
        hop_half(slot, z, 1, 8, down).wait_send()
        to_sibling_half(slot, z, 0, 4).wait_send()
        to_sibling_half(slot, z, 1, 8).wait_send()

    sent(0)
    sent(2)

    @pl.when(outer == 1)
    def _():
        sent(3)

    @pl.when(y == 2)
    def _():
        late_to_near().wait_send()
        for i, ref in enumerate((k_ref, v_ref)):
            across_copy(i, ref).wait_send()

    def near_sent(k, carry):
        to_near(z, k).wait_send()
        to_near(z, k + 4).wait_send()
        to_sibling(1, z, k).wait_send()
        to_sibling(1, z, k + 4).wait_send()
        return carry

    lax.fori_loop(1, 4, near_sent, 0)
    to_near(z, 0).wait_send()
    to_sibling(1, z, 0).wait_send()
    to_near_half(z, 0, 4).wait_send()
    to_near_half(z, 1, 8).wait_send()
    to_sibling_half(1, z, 0, 4).wait_send()
    to_sibling_half(1, z, 1, 8).wait_send()


def local(queries, key_states, value_states, out_weight):
    bf16, f32 = jnp.bfloat16, jnp.float32
    any_spec = pl.BlockSpec(memory_space=pl.ANY)
    dma = pltpu.SemaphoreType.DMA
    share, from_below, from_above = pl.pallas_call(
        kernel,
        out_shape=[jax.ShapeDtypeStruct((T, 1024), bf16)] * 3,
        in_specs=[any_spec] * 4,
        out_specs=[any_spec] * 3,
        scratch_shapes=[
            pltpu.VMEM((4, Z, 2, U, HEAD_DIM), bf16),
            pltpu.VMEM((2, U, 256), bf16),
            pltpu.VMEM((2, ROWS, 256), bf16),
            pltpu.VMEM((2, ROWS, 256), f32),
            pltpu.VMEM((2, ROWS, HEAD_DIM), f32),
            pltpu.VMEM((2, U, 256), bf16),
            pltpu.VMEM((T, 1024), bf16),
            pltpu.VMEM((4, 1024, 1024), bf16),
            pltpu.VMEM((2, T, 1024), bf16),
            pltpu.VMEM((T, 1024), bf16),
            pltpu.VMEM((T, 1024), bf16),
            pltpu.VMEM((2, T, 512), bf16),
            dma((4, 9)), dma((4, 9)), dma((4, 9)), dma((4, 9)),
            dma((10,)), dma((2,)), dma((2,)), dma((2,)),
            dma, dma((3,)), dma((3,)), dma((2,)), dma((2,)), dma((4,)),
            dma((3, 2)), dma((3, 2)), dma((2,)), dma((6, 2)), dma((6, 2)), dma,
        ],
        compiler_params=pltpu.CompilerParams(
            collective_id=0, has_side_effects=True, vmem_limit_bytes=60 << 20
        ),
    )(queries, key_states, value_states, out_weight)
    return (share.astype(f32) + from_below.astype(f32) + from_above.astype(f32)).astype(bf16)


def solution(mesh):
    return jax.shard_map(
        local,
        mesh=mesh,
        in_specs=(P("seq", "head"), P("seq", "head"), P("seq", "head"), P("head", None)),
        out_specs=P("seq", "head"),
        check_vma=False,
    )
```
